512 devices in a mesh: tile: 64 (over z, y_hi, core), mem: 8 (over x, y_lo).
Axes of the slice: x: 4, y: 4 (y_hi: 2, y_lo: 2; y = y_hi * 2 + y_lo), z: 16, core: 2. Of those that a mesh axis runs over, the one named last changes fastest.
Arguments:
- member_tracer_state: float32 [64, 8, 16, 16384], P('mem', None, None, 'tile'), may hold values from -6 to 6
- diffusivity: float32 [4, 16, 16384], P(None, None, 'tile'), may hold values from 0.02 to 0.15
- velocity: float32 [4, 16, 16384], P(None, None, 'tile'), may hold values from -0.4 to 0.4
- wet_mask: int32 [16, 16384], P(None, 'tile'), may hold values from 0 to 1, as said below
- obs_cell: int32 [8192], P('tile'), may hold values from 0 to 4095, as said below
- obs_count: int32 [64], P('tile'), may hold values from 1 to 128, as said below
- obs_value: float32 [8192], P('tile'), may hold values from -6 to 6
- obs_error: float32 [8192], P('tile'), may hold values from 0.2 to 1
Outputs:
- analysis: float32 [64, 8, 16, 16384], P('mem', None, None, 'tile')
The draws below stay inside these ranges and needn't reach their ends.
Inputs may be any that keep to these rules, and one draw needn't show every extreme that they name: `wet_mask`: 1 marks an ocean cell, 0 land; every block of 256 columns has some ocean cells and at least one block is all ocean. `obs_count`: how many of a block's 128 slots are in use; one block uses all of them. `obs_cell`: a cell of the block as row * 256 + column; the slots of a block are distinct cells, and those in use are ocean cells.
All inputs are finite; a program needn't handle non-finite values.
Results may differ from the reference program's by a relative error of at most 0.00018.
Values sent between devices are 32-bit elements; how exact they have to be, the bound alone decides.
No kernel may reach another device: no remote copies, remote signals or barrier semaphores. Data moves between devices by JAX's collectives and lax.ppermute only.
A program may use at most 64 MiB of HBM per device.

```python
import math
import jax
import jax.numpy as jnp
from jax import lax

BAND_ROWS = 16
BLOCK_WIDTH = 256
LEVEL_COUNT = 4
OBS_DEV = 128
MEMBER_COUNT = 64
NLON = 16384
NOBS = 8192


def layout(key):
    column_blocks = NLON // BLOCK_WIDTH
    cell_total = BAND_ROWS * BLOCK_WIDTH
    land_key, cell_key, pick_key, order_key = jax.random.split(key, 4)
    land_share = jax.random.randint(land_key, (column_blocks,), 0, 60)
    open_block = jax.random.randint(pick_key, (), 0, column_blocks)
    land_share = jnp.where(jnp.arange(column_blocks) == open_block, 0, land_share)
    dice_rolls = jax.random.randint(cell_key, (column_blocks, cell_total), 0, 100)
    wet_flag = (dice_rolls >= land_share[:, None]).astype(jnp.int32)
    shuffle = jax.vmap(lambda one_key: jax.random.permutation(one_key, cell_total))(jax.random.split(order_key, column_blocks))
    ranking = wet_flag * cell_total + shuffle.astype(jnp.int32)
    chosen = lax.top_k(ranking, OBS_DEV)[1].astype(jnp.int32)
    wet_total = jnp.sum(wet_flag, 1)
    in_use = jnp.maximum(wet_total * OBS_DEV // cell_total, 1).astype(jnp.int32)
    return (wet_flag, chosen, in_use)


def draw_wet_mask(key, part):
    wet_flag, chosen, in_use = layout(key)
    column_blocks = NLON // BLOCK_WIDTH
    return wet_flag.reshape(column_blocks, BAND_ROWS, BLOCK_WIDTH).transpose(1, 0, 2).reshape(BAND_ROWS, NLON)


def draw_obs_cell(key, part):
    wet_flag, chosen, in_use = layout(key)
    return chosen.reshape(-1)


def draw_obs_count(key, part):
    wet_flag, chosen, in_use = layout(key)
    return in_use


def steps_of(own_key, extent, shards, smallest, high):
    def one(position, parts):
        heights = jax.random.uniform(jax.random.fold_in(jax.random.fold_in(own_key, 6), position), (parts,), jnp.float32, smallest / len(shards), high / len(shards))
        return jnp.repeat(jnp.exp(heights), extent[position] // parts).reshape((-1,) + (1,) * (len(extent) - position - 1))

    gain = one(*shards[0])
    for cut in shards[1:]:
        gain = gain * one(*cut)
    return gain


def scatter_about(own_key, extent, deviation, limit, cuts=(), held_as=jnp.bfloat16):
    result = jax.random.normal(own_key, extent, jnp.float32) * deviation
    if len(cuts) > 0:
        result = steps_of(own_key, extent, cuts, -0.22, 0.18) * result
    return jnp.clip(result, min=-limit, max=limit).astype(held_as)


def setup_inputs(seed: int = 0) -> dict:
    streams_of = jax.random.split(jax.random.key(seed), 9)
    member_tracer_state = scatter_about(streams_of[0], (MEMBER_COUNT, 2 * LEVEL_COUNT, BAND_ROWS, NLON), 1.0, 6.0, ((0, 8), (3, 64)), jnp.float32)
    diffusivity = jnp.clip(jnp.exp(math.log(0.15) - 2.014903 * jax.random.uniform(streams_of[1], (LEVEL_COUNT, BAND_ROWS, NLON), jnp.float32) ** steps_of(streams_of[1], (LEVEL_COUNT, BAND_ROWS, NLON), ((2, 64),), -0.2, 0.2)), 0.02, 0.15)
    velocity = jnp.clip(jax.random.uniform(streams_of[2], (LEVEL_COUNT, BAND_ROWS, NLON), jnp.float32, -0.4, 0.4) * steps_of(streams_of[2], (LEVEL_COUNT, BAND_ROWS, NLON), ((2, 64),), -0.4, 0.0), -0.4, 0.4)
    wet_mask = draw_wet_mask(jax.random.fold_in(streams_of[8], 71), 0)
    obs_cell = draw_obs_cell(jax.random.fold_in(streams_of[8], 71), 0)
    obs_count = draw_obs_count(jax.random.fold_in(streams_of[8], 71), 0)
    obs_value = scatter_about(streams_of[6], (NOBS,), 1.0, 6.0, ((0, 64),), jnp.float32)
    obs_error = jnp.clip(jnp.exp(math.log(1.0) - 1.609438 * jax.random.uniform(streams_of[7], (NOBS,), jnp.float32) ** steps_of(streams_of[7], (NOBS,), ((0, 64),), -0.2, 0.2)), 0.2, 1.0)
    return {"member_tracer_state": member_tracer_state, "diffusivity": diffusivity, "velocity": velocity, "wet_mask": wet_mask, "obs_cell": obs_cell, "obs_count": obs_count, "obs_value": obs_value, "obs_error": obs_error}


def advect_tracers(padded_state, statics):
    levels = (statics.shape[0] - 1) // 2
    diffuse = statics[:levels]
    velocity = statics[levels:2 * levels]
    wet_flag = statics[2 * levels]
    member_index = padded_state.shape[0]
    latitude_rows = padded_state.shape[2]
    grid_columns = padded_state.shape[3]
    tracer_field = padded_state.reshape(member_index, 2, levels, latitude_rows, grid_columns)
    west_cells = tracer_field[..., :-1]
    east_cells = tracer_field[..., 1:]
    face_diffuse = 0.5 * (diffuse[..., :-1] + diffuse[..., 1:])
    face_speed = 0.5 * (velocity[..., :-1] + velocity[..., 1:])
    face_wet = wet_flag[:, :-1] * wet_flag[:, 1:]
    zonal_flux = face_wet * (jnp.maximum(face_speed, 0.0) * west_cells + jnp.minimum(face_speed, 0.0) * east_cells - face_diffuse * (east_cells - west_cells))
    middle = tracer_field[..., 1:-1]
    inner_diffuse = diffuse[..., 1:-1]
    inner_wet = wet_flag[:, 1:-1]
    north_diffuse = 0.5 * (inner_diffuse[:, :-1] + inner_diffuse[:, 1:])
    north_wet = inner_wet[:-1] * inner_wet[1:]
    north_flux = -north_wet * north_diffuse * (middle[..., 1:, :] - middle[..., :-1, :])
    zero_row = jnp.zeros_like(middle[..., :1, :])
    outflow = jnp.concatenate([north_flux, zero_row], 3)
    inflow = jnp.concatenate([zero_row, north_flux], 3)
    change = zonal_flux[..., :-1] - zonal_flux[..., 1:] + inflow - outflow
    updated = middle + inner_wet * change
    return updated.reshape(member_index, 2 * levels, latitude_rows, grid_columns - 2)

def coefficients(observed, obs_value, obs_error, in_use, locality):
    ens_size = observed.shape[0]
    ens_mean = jnp.sum(observed, 0) / ens_size
    anomaly = (observed - ens_mean) * in_use
    innovation = (obs_value - ens_mean) * in_use
    system = jnp.dot(anomaly.T, anomaly, precision=lax.Precision.HIGHEST) + (ens_size - 1) * jnp.diag(obs_error / locality)
    factor = jnp.linalg.cholesky(system)
    right_sides = jnp.concatenate([innovation[:, None], anomaly.T], 1)
    solved = jax.scipy.linalg.cho_solve((factor, True), right_sides)
    mixed = jnp.dot(anomaly, solved, precision=lax.Precision.HIGHEST)
    return mixed[:, :1] - 0.5 * mixed[:, 1:]

def near_slots(values):
    return jnp.concatenate([jnp.roll(values, 1, -2), values, jnp.roll(values, -1, -2)], -1)

def reference(member_tracer_state, diffusivity, velocity, wet_mask, obs_cell, obs_count, obs_value, obs_error):
    statics = jnp.concatenate([diffusivity, velocity, wet_mask.astype(jnp.float32)[None]], 0)
    periodic_state = jnp.concatenate([statics[..., -1:], statics, statics[..., :1]], 2)
    prior_state = member_tracer_state
    for sweep_number in range(2):
        padded_state = jnp.concatenate([prior_state[..., -1:], prior_state, prior_state[..., :1]], 3)
        prior_state = advect_tracers(padded_state, periodic_state)
    column_blocks = NLON // BLOCK_WIDTH
    surface_level = prior_state[:, 0].reshape(MEMBER_COUNT, BAND_ROWS, column_blocks, BLOCK_WIDTH).transpose(0, 2, 1, 3).reshape(MEMBER_COUNT, column_blocks, BAND_ROWS * BLOCK_WIDTH)
    slot_cells = jnp.broadcast_to(obs_cell.reshape(column_blocks, OBS_DEV)[None], (MEMBER_COUNT, column_blocks, OBS_DEV))
    observed = jnp.take_along_axis(surface_level, slot_cells, axis=2)
    in_use = (jnp.arange(OBS_DEV, dtype=jnp.int32)[None, :] < obs_count[:, None]).astype(jnp.float32)
    locality = jnp.concatenate([jnp.full((OBS_DEV,), 0.5, jnp.float32), jnp.ones((OBS_DEV,), jnp.float32), jnp.full((OBS_DEV,), 0.5, jnp.float32)])
    near_obs = near_slots(observed).transpose(1, 0, 2)
    near_value = near_slots(obs_value.reshape(column_blocks, OBS_DEV))
    near_error = near_slots(obs_error.reshape(column_blocks, OBS_DEV))
    near_use = near_slots(in_use)
    weights = lax.map(lambda items: coefficients(items[0], items[1], items[2], items[3], locality), (near_obs, near_value, near_error, near_use))
    blocked_state = prior_state.reshape(MEMBER_COUNT, 2 * LEVEL_COUNT, BAND_ROWS, column_blocks, BLOCK_WIDTH)
    analysis_change = jnp.einsum('bke,kqrbc->eqrbc', weights, blocked_state, precision=lax.Precision.HIGHEST)
    return (blocked_state + analysis_change).reshape(MEMBER_COUNT, 2 * LEVEL_COUNT, BAND_ROWS, NLON)
```

```python
import jax
import jax.numpy as jnp
from jax import lax
from jax.experimental import pallas as pl
from jax.experimental.pallas import tpu as pltpu
from jax.sharding import PartitionSpec as P

LEVELS = 4
PLANES = 8
MEMBERS = 8
ENSEMBLE = 64
ROWS = 16
COLUMNS = 256
SLOTS = 128
LANES = 128
HALF_ROWS = ROWS * MEMBERS
CELL_ROWS = 2 * HALF_ROWS
CHUNK_ROWS = CELL_ROWS + MEMBERS
SYSTEM_ROWS = ENSEMBLE + 8
HIGHEST = lax.Precision.HIGHEST
PARAMS = pltpu.CompilerParams(vmem_limit_bytes=32 * 1024 * 1024)


def lane_index(shape):
    return lax.broadcasted_iota(jnp.int32, shape, 1)


def pack_edges(state, diffusivity, velocity, wet, first, last):
    pair = lane_index((ROWS, LANES)) >> 1

    def put(low, high, index, kept):
        first_kept, last_kept = kept
        first_kept = jnp.where(pair == index, pltpu.roll(low, 2 * index, 1), first_kept)
        last_kept = jnp.where(
            pair == index, pltpu.roll(high, (2 * index + 2) % LANES, 1), last_kept
        )
        return first_kept, last_kept

    zeros = jnp.zeros((ROWS, LANES), jnp.float32)

    def member(e, kept):
        for q in range(PLANES):
            kept = put(state[e, q, :, :LANES], state[e, q, :, LANES:], e * PLANES + q, kept)
        return kept

    kept = lax.fori_loop(0, MEMBERS, member, (zeros, zeros))
    first[:, :LANES], last[:, :LANES] = kept
    kept = (zeros, zeros)
    for level in range(LEVELS):
        kept = put(diffusivity[level, :, :LANES], diffusivity[level, :, LANES:], level, kept)
        kept = put(velocity[level, :, :LANES], velocity[level, :, LANES:], LEVELS + level, kept)
    flags = wet[...].astype(jnp.float32)
    kept = put(flags[:, :LANES], flags[:, LANES:], 2 * LEVELS, kept)
    first[:, LANES:], last[:, LANES:] = kept


def from_west(tiles):
    lane = lane_index((ROWS, LANES))
    turned = [pltpu.roll(tile, 1, 1) for tile in tiles]
    return [jnp.where(lane == 0, turned[i - 1], turned[i]) for i in range(3)]


def from_east(tiles):
    lane = lane_index((ROWS, LANES))
    turned = [pltpu.roll(tile, LANES - 1, 1) for tile in tiles]
    return [jnp.where(lane == LANES - 1, turned[(i + 1) % 3], turned[i]) for i in range(3)]


def halo_tile(west, east, index):
    lane = lane_index((ROWS, LANES))
    east = pltpu.roll(east, (LANES - 2 * index) % LANES, 1)
    west = pltpu.roll(west, LANES - 2 - 2 * index, 1)
    return jnp.where(lane < 2, east, jnp.where(lane >= LANES - 2, west, 0.0))


def transport(
    state, diffusivity, velocity, wet, west_halo, east_halo, obs_cell, chunks
):
    row = lax.broadcasted_iota(jnp.int32, (ROWS, LANES), 0)
    flags = wet[...].astype(jnp.float32)

    def widened(block, index, lanes):
        return [
            block[:, :LANES],
            block[:, LANES:],
            halo_tile(west_halo[:, lanes], east_halo[:, lanes], index),
        ]

    tracer_lanes, static_lanes = slice(0, LANES), slice(LANES, 2 * LANES)
    ocean = widened(flags, 2 * LEVELS, static_lanes)
    ocean_west = from_west(ocean)
    ocean_south = [pltpu.roll(x, ROWS - 1, 0) for x in ocean]

    def level_step(level, carry):
        diffuse = widened(diffusivity[level], level, static_lanes)
        speed = widened(velocity[level], LEVELS + level, static_lanes)
        diffuse_west, speed_west = from_west(diffuse), from_west(speed)
        face_west, face_east, north = [], [], []
        for i in range(3):
            face = ocean_west[i] * ocean[i]
            a = 0.5 * (speed_west[i] + speed[i])
            k = 0.5 * (diffuse_west[i] + diffuse[i])
            face_west.append(face * (jnp.maximum(a, 0.0) + k))
            face_east.append(face * (jnp.minimum(a, 0.0) - k))
            k = 0.5 * (diffuse[i] + pltpu.roll(diffuse[i], ROWS - 1, 0))
            north.append(jnp.where(row < ROWS - 1, ocean[i] * ocean_south[i] * k, 0.0))
        next_west, next_east = from_east(face_west), from_east(face_east)
        above = [pltpu.roll(x, 1, 0) for x in north]
        centre = [
            1.0 + (face_east[i] - next_west[i] - above[i] - north[i]) * ocean[i]
            for i in range(3)
        ]

        def advance(tiles, count):
            west, east = from_west(tiles), from_east(tiles)
            return [
                centre[i] * tiles[i]
                + face_west[i] * west[i]
                - next_east[i] * east[i]
                + above[i] * pltpu.roll(tiles[i], 1, 0)
                + north[i] * pltpu.roll(tiles[i], ROWS - 1, 0)
                for i in range(count)
            ]

        def member_step(e, carry):
            for tracer in range(2):
                q = tracer * LEVELS + level
                tiles = widened(state[e, q], e * PLANES + q, tracer_lanes)
                done = advance(advance(tiles, 3), 2)
                for half in range(2):
                    rows = pl.ds(half * HALF_ROWS + e, ROWS, stride=MEMBERS)
                    chunks[q, rows, :] = done[half]
            return carry

        return lax.fori_loop(0, MEMBERS, member_step, carry)

    lax.fori_loop(0, LEVELS, level_step, 0)
    cell = obs_cell[...]
    column = lax.broadcasted_iota(jnp.int32, (COLUMNS, SLOTS), 0)
    pick = (column == (cell & (COLUMNS - 1))).astype(jnp.float32)
    surface = jnp.concatenate([chunks[0, :HALF_ROWS, :], chunks[0, HALF_ROWS:CELL_ROWS, :]], 1)
    near = jnp.dot(
        surface, pick, precision=HIGHEST, preferred_element_type=jnp.float32
    ).reshape(ROWS, MEMBERS, SLOTS)
    layer = lax.broadcasted_iota(jnp.int32, (ROWS, MEMBERS, SLOTS), 0)
    observed = jnp.sum(jnp.where(layer == (cell >> 8)[None], near, 0.0), 0)
    for q in range(PLANES):
        chunks[q, CELL_ROWS:, :] = observed


def block_system(observed, obs_count, obs_value, obs_error, out):
    members = observed[...].reshape(ENSEMBLE, SLOTS)
    slot = lane_index((1, SLOTS))
    in_use = (slot < obs_count[0]).astype(jnp.float32)
    mean = jnp.sum(members, 0, keepdims=True) / ENSEMBLE
    anomaly = (members - mean) * in_use
    innovation = (obs_value[...] - mean) * in_use
    scaled = anomaly / ((ENSEMBLE - 1) * obs_error[...])
    first = lax.broadcasted_iota(jnp.int32, (8, SLOTS), 0) == 0
    left = jnp.concatenate([anomaly, jnp.where(first, innovation, 0.0)], 0)
    right = jnp.concatenate([scaled, jnp.zeros((LANES - ENSEMBLE, SLOTS), jnp.float32)], 0)
    out[...] = lax.dot_general(
        left, right, (((1,), (1,)), ((), ())), precision=HIGHEST,
        preferred_element_type=jnp.float32,
    )


def inverse(system):
    row = lax.broadcasted_iota(jnp.int32, (SYSTEM_ROWS, LANES), 0)
    lane = lane_index((SYSTEM_ROWS, LANES))
    for k in range(ENSEMBLE):
        pivot_row = system[k : k + 1, :]
        scale = 1.0 / pivot_row[:, k : k + 1]
        scaled = jnp.where(lane[:1] == k, scale, pivot_row * scale)
        column = system[:, k : k + 1]
        rest = jnp.where(lane == k, 0.0, system)
        system = jnp.where(row == k, scaled, rest - column * scaled)
    return system


def update(own, west, east, received, out):
    row = lax.broadcasted_iota(jnp.int32, (SYSTEM_ROWS, LANES), 0)
    diagonal = row == lane_index((SYSTEM_ROWS, LANES))
    identity = jnp.where(diagonal & (row < ENSEMBLE), 1.0, 0.0)
    solved = inverse(identity + own[...] + 0.5 * (west[...] + east[...]))
    weights = 0.5 * (identity + solved)[:ENSEMBLE] - solved[ENSEMBLE : ENSEMBLE + 1]
    weights = weights[:, :ENSEMBLE]
    for r in range(ROWS):
        halves = [
            received[:, first : first + MEMBERS, :].reshape(ENSEMBLE, LANES)
            for first in (r * MEMBERS, HALF_ROWS + r * MEMBERS)
        ]
        result = jnp.dot(
            weights, jnp.concatenate(halves, 1), precision=HIGHEST,
            preferred_element_type=jnp.float32,
        )
        for m in range(ENSEMBLE // MEMBERS):
            rows = result[m * MEMBERS : (m + 1) * MEMBERS]
            out[m, pl.ds(r, MEMBERS, stride=ROWS), :] = rows[:, :LANES]
            out[m, pl.ds(HALF_ROWS + r, MEMBERS, stride=ROWS), :] = rows[:, LANES:]


def unpack(planes, out):
    for q in range(planes.shape[0]):
        out[:, q, :, :LANES] = planes[q, :HALF_ROWS, :].reshape(MEMBERS, ROWS, LANES)
        out[:, q, :, LANES:] = planes[q, HALF_ROWS:, :].reshape(MEMBERS, ROWS, LANES)


def vmem():
    return pl.BlockSpec(memory_space=pltpu.VMEM)


def shifted(value, step):
    count = lax.axis_size("tile")
    return lax.ppermute(value, "tile", [(i, (i + step) % count) for i in range(count)])


def local(
    member_tracer_state, diffusivity, velocity, wet_mask, obs_cell, obs_count, obs_value, obs_error
):
    edge = jax.ShapeDtypeStruct((ROWS, COLUMNS), jnp.float32)
    first, last = pl.pallas_call(
        pack_edges,
        out_shape=(edge, edge),
        in_specs=[vmem()] * 4,
        out_specs=(vmem(), vmem()),
        compiler_params=PARAMS,
        name="pack_edges",
    )(member_tracer_state, diffusivity, velocity, wet_mask)
    west_halo = shifted(last, 1)
    east_halo = shifted(first, -1)
    chunks = pl.pallas_call(
        transport,
        out_shape=jax.ShapeDtypeStruct((PLANES, CHUNK_ROWS, LANES), jnp.float32),
        in_specs=[vmem()] * 7,
        out_specs=vmem(),
        compiler_params=PARAMS,
        name="transport",
    )(
        member_tracer_state, diffusivity, velocity, wet_mask, west_halo, east_halo,
        obs_cell.reshape(1, SLOTS),
    )
    received = lax.all_to_all(chunks, "mem", split_axis=0, concat_axis=0, tiled=True)
    share = pl.pallas_call(
        block_system,
        out_shape=jax.ShapeDtypeStruct((SYSTEM_ROWS, LANES), jnp.float32),
        grid=(1,),
        in_specs=[
            pl.BlockSpec((PLANES, MEMBERS, SLOTS), lambda i: (0, CELL_ROWS // MEMBERS, 0)),
            pl.BlockSpec(memory_space=pltpu.SMEM),
            pl.BlockSpec((1, SLOTS), lambda i: (0, 0)),
            pl.BlockSpec((1, SLOTS), lambda i: (0, 0)),
        ],
        out_specs=pl.BlockSpec((SYSTEM_ROWS, LANES), lambda i: (0, 0)),
        compiler_params=PARAMS,
        name="block_system",
    )(received, obs_count, obs_value.reshape(1, SLOTS), obs_error.reshape(1, SLOTS))
    west_share = shifted(share, 1)
    east_share = shifted(share, -1)
    updated = pl.pallas_call(
        update,
        out_shape=jax.ShapeDtypeStruct((PLANES, CELL_ROWS, LANES), jnp.float32),
        in_specs=[vmem()] * 4,
        out_specs=vmem(),
        compiler_params=PARAMS,
        name="update",
    )(share, west_share, east_share, received)
    back = lax.all_to_all(updated, "mem", split_axis=0, concat_axis=0, tiled=True)
    return pl.pallas_call(
        unpack,
        out_shape=jax.ShapeDtypeStruct(member_tracer_state.shape, jnp.float32),
        grid=(2,),
        in_specs=[pl.BlockSpec((PLANES // 2, CELL_ROWS, LANES), lambda i: (i, 0, 0))],
        out_specs=pl.BlockSpec(
            (MEMBERS, PLANES // 2, ROWS, COLUMNS), lambda i: (0, i, 0, 0)
        ),
        compiler_params=PARAMS,
        name="unpack",
    )(back)


def solution(mesh):
    in_specs = (
        P("mem", None, None, "tile"),
        P(None, None, "tile"),
        P(None, None, "tile"),
        P(None, "tile"),
        P("tile"),
        P("tile"),
        P("tile"),
        P("tile"),
    )
    out_specs = P("mem", None, None, "tile")
    return jax.shard_map(local, mesh=mesh, in_specs=in_specs, out_specs=out_specs, check_vma=False)
```

```python
import jax
import jax.numpy as jnp
from jax import lax
from jax.experimental import pallas as pl
from jax.experimental.pallas import tpu as pltpu
from jax.sharding import PartitionSpec as P

LEVELS = 4
PLANES = 8
MEMBERS = 8
ENSEMBLE = 64
ROWS = 16
COLUMNS = 256
SLOTS = 128
LANES = 128
HALF_ROWS = ROWS * MEMBERS
CELL_ROWS = 2 * HALF_ROWS
SYSTEM_ROWS = ENSEMBLE + 8
HIGHEST = lax.Precision.HIGHEST
PARAMS = pltpu.CompilerParams(vmem_limit_bytes=32 * 1024 * 1024)


def lane_index(shape):
    return lax.broadcasted_iota(jnp.int32, shape, 1)


def pack_edges(
    state, diffusivity, velocity, wet, first, last, own_state, own_statics, own_wet, arrived
):
    copies = [
        pltpu.make_async_copy(diffusivity, own_statics.at[:LEVELS], arrived.at[0]),
        pltpu.make_async_copy(velocity, own_statics.at[LEVELS:], arrived.at[1]),
        pltpu.make_async_copy(wet, own_wet, arrived.at[2]),
    ]
    for part in range(2):
        rows = slice(part * MEMBERS // 2, (part + 1) * MEMBERS // 2)
        copies.append(
            pltpu.make_async_copy(state.at[rows], own_state.at[rows], arrived.at[3 + part])
        )
    for copy in copies:
        copy.start()
    pair = lane_index((ROWS, LANES)) >> 1

    def put(low, high, index, kept):
        first_kept, last_kept = kept
        first_kept = jnp.where(pair == index, pltpu.roll(low, 2 * index, 1), first_kept)
        last_kept = jnp.where(
            pair == index, pltpu.roll(high, (2 * index + 2) % LANES, 1), last_kept
        )
        return first_kept, last_kept

    zeros = jnp.zeros((ROWS, LANES), jnp.float32)
    kept = (zeros, zeros)
    for copy in copies[:3]:
        copy.wait()
    for i in range(2 * LEVELS):
        kept = put(own_statics[i, :, :LANES], own_statics[i, :, LANES:], i, kept)
    flags = own_wet[...].astype(jnp.float32)
    kept = put(flags[:, :LANES], flags[:, LANES:], 2 * LEVELS, kept)
    first[:, LANES:], last[:, LANES:] = kept

    def member(e, kept):
        for q in range(PLANES):
            low, high = own_state[e, q, :, :LANES], own_state[e, q, :, LANES:]
            kept = put(low, high, e * PLANES + q, kept)
        return kept

    kept = (zeros, zeros)
    for part in range(2):
        copies[3 + part].wait()
        kept = lax.fori_loop(part * MEMBERS // 2, (part + 1) * MEMBERS // 2, member, kept)
    first[:, :LANES], last[:, :LANES] = kept


def from_west(tiles):
    lane = lane_index((ROWS, LANES))
    turned = [pltpu.roll(tile, 1, 1) for tile in tiles]
    return [jnp.where(lane == 0, turned[i - 1], turned[i]) for i in range(3)]


def from_east(tiles):
    lane = lane_index((ROWS, LANES))
    turned = [pltpu.roll(tile, LANES - 1, 1) for tile in tiles]
    return [jnp.where(lane == LANES - 1, turned[(i + 1) % 3], turned[i]) for i in range(3)]


def halo_tile(west, east, index):
    lane = lane_index((ROWS, LANES))
    east = pltpu.roll(east, (LANES - 2 * index) % LANES, 1)
    west = pltpu.roll(west, LANES - 2 - 2 * index, 1)
    return jnp.where(lane < 2, east, jnp.where(lane >= LANES - 2, west, 0.0))


TRACER_LANES, STATIC_LANES = slice(0, LANES), slice(LANES, 2 * LANES)


def widened(block, west_halo, east_halo, lanes, index):
    halo = halo_tile(west_halo[:, lanes], east_halo[:, lanes], index)
    return [block[:, :LANES], block[:, LANES:], halo]


def stepper(level, statics, wet, west_halo, east_halo):
    row = lax.broadcasted_iota(jnp.int32, (ROWS, LANES), 0)
    halos = (west_halo, east_halo, STATIC_LANES)
    ocean = widened(wet[...].astype(jnp.float32), *halos, 2 * LEVELS)
    diffuse = widened(statics[level], *halos, level)
    speed = widened(statics[LEVELS + level], *halos, LEVELS + level)
    ocean_west, diffuse_west, speed_west = map(from_west, (ocean, diffuse, speed))
    face_west, face_east, north = [], [], []
    for i in range(3):
        face = ocean_west[i] * ocean[i]
        a = 0.5 * (speed_west[i] + speed[i])
        k = 0.5 * (diffuse_west[i] + diffuse[i])
        face_west.append(face * (jnp.maximum(a, 0.0) + k))
        face_east.append(face * (jnp.minimum(a, 0.0) - k))
        k = 0.5 * (diffuse[i] + pltpu.roll(diffuse[i], ROWS - 1, 0))
        both = ocean[i] * pltpu.roll(ocean[i], ROWS - 1, 0)
        north.append(jnp.where(row < ROWS - 1, both * k, 0.0))
    next_west, next_east = from_east(face_west), from_east(face_east)
    above = [pltpu.roll(x, 1, 0) for x in north]
    centre = [
        1.0 + (face_east[i] - next_west[i] - above[i] - north[i]) * ocean[i] for i in range(3)
    ]

    def advance(tiles, count):
        west, east = from_west(tiles), from_east(tiles)
        return [
            centre[i] * tiles[i]
            + face_west[i] * west[i]
            - next_east[i] * east[i]
            + above[i] * pltpu.roll(tiles[i], 1, 0)
            + north[i] * pltpu.roll(tiles[i], ROWS - 1, 0)
            for i in range(count)
        ]

    return lambda tiles: advance(advance(tiles, 3), 2)


def transport(state, statics, wet, west_halo, east_halo, chunks):
    def level_step(level, carry):
        steps = stepper(level, statics, wet, west_halo, east_halo)

        def member_step(e, carry):
            for tracer in range(2):
                q = tracer * LEVELS + level
                done = steps(
                    widened(state[e, q], west_halo, east_halo, TRACER_LANES, e * PLANES + q)
                )
                for half in range(2):
                    rows = pl.ds(half * HALF_ROWS + e, ROWS, stride=MEMBERS)
                    chunks[q, rows, :] = done[half]
            return carry

        return lax.fori_loop(0, MEMBERS, member_step, carry, unroll=4)

    lax.fori_loop(0, LEVELS, level_step, 0)


def observe(
    state, statics, wet, west_halo, east_halo, count, cell, value, error, out, slots,
    own_cell, own_value, own_error, arrived
):
    copies = [
        pltpu.make_async_copy(cell, own_cell, arrived.at[0]),
        pltpu.make_async_copy(value, own_value, arrived.at[1]),
        pltpu.make_async_copy(error, own_error, arrived.at[2]),
    ]
    for copy in copies:
        copy.start()
    steps = stepper(0, statics, wet, west_halo, east_halo)
    surface = []
    for e in range(MEMBERS):
        done = steps(widened(state[e, 0], west_halo, east_halo, TRACER_LANES, e * PLANES))
        surface.append(jnp.concatenate(done, 1))
    for copy in copies:
        copy.wait()
    in_use = (lane_index((1, SLOTS)) < count[0]).astype(jnp.float32)
    scale = 1.0 / ((ENSEMBLE - 1) * own_error[...])
    unused = jnp.zeros((5, SLOTS), jnp.float32)
    slots[...] = jnp.concatenate([in_use, own_value[...], scale, unused], 0)
    cell = own_cell[...]
    column = lax.broadcasted_iota(jnp.int32, (COLUMNS, SLOTS), 0)
    pick = (column == (cell & (COLUMNS - 1))).astype(jnp.float32)
    near = jnp.dot(
        jnp.concatenate(surface, 0), pick, precision=HIGHEST, preferred_element_type=jnp.float32
    )
    layer = lax.broadcasted_iota(jnp.int32, (ROWS, SLOTS), 0)
    chosen = layer == (cell >> 8)
    for e in range(MEMBERS):
        kept = jnp.where(chosen, near[e * ROWS : (e + 1) * ROWS], 0.0)
        picked = jnp.sum(kept, 0, keepdims=True)
        for m in range(ENSEMBLE // MEMBERS):
            out[m, e : e + 1, :] = picked


def block_system(observed, slots, out):
    members = observed[...].reshape(ENSEMBLE, SLOTS)
    in_use, value, scale = slots[0:1], slots[1:2], slots[2:3]
    mean = jnp.sum(members, 0, keepdims=True) / ENSEMBLE
    anomaly = (members - mean) * in_use
    innovation = (value - mean) * in_use
    first = lax.broadcasted_iota(jnp.int32, (8, SLOTS), 0) == 0
    left = jnp.concatenate([anomaly, jnp.where(first, innovation, 0.0)], 0)
    unused = jnp.zeros((LANES - ENSEMBLE, SLOTS), jnp.float32)
    right = jnp.concatenate([anomaly * scale, unused], 0)
    out[...] = lax.dot_general(
        left, right, (((1,), (1,)), ((), ())), precision=HIGHEST,
        preferred_element_type=jnp.float32,
    )


def symmetric_inverse(a, b, c):
    scale = 1.0 / (a * c - b * b)
    return c * scale, -b * scale, a * scale


def pivot_inverse(e):
    a0, a1, a2 = symmetric_inverse(e[0][0], e[0][1], e[1][1])
    b00, b01, b10, b11 = e[0][2], e[0][3], e[1][2], e[1][3]
    f00, f01 = a0 * b00 + a1 * b10, a0 * b01 + a1 * b11
    f10, f11 = a1 * b00 + a2 * b10, a1 * b01 + a2 * b11
    s0, s1, s2 = symmetric_inverse(
        e[2][2] - (b00 * f00 + b10 * f10),
        e[2][3] - (b00 * f01 + b10 * f11),
        e[3][3] - (b01 * f01 + b11 * f11),
    )
    t00, t01 = f00 * s0 + f01 * s1, f00 * s1 + f01 * s2
    t10, t11 = f10 * s0 + f11 * s1, f10 * s1 + f11 * s2
    x01 = a1 + t00 * f10 + t01 * f11
    return [
        [a0 + t00 * f00 + t01 * f01, x01, -t00, -t01],
        [x01, a2 + t10 * f10 + t11 * f11, -t10, -t11],
        [-t00, -t10, s0, s1],
        [-t01, -t11, s1, s2],
    ]


def inverse(tiles):
    row = lax.broadcasted_iota(jnp.int32, (8, LANES), 0)
    lane = lane_index((8, LANES))
    size = 4

    def everywhere(block):
        return jnp.broadcast_to(block, (8, LANES))

    for k in range(0, ENSEMBLE, size):
        home, start = k // 8, k % 8
        columns = [[everywhere(tile[:, k + j : k + j + 1]) for tile in tiles] for j in range(size)]
        rows = [everywhere(tiles[home][start + i : start + i + 1]) for i in range(size)]
        pivots = pivot_inverse(
            [
                [everywhere(columns[j][home][start + i : start + i + 1]) for j in range(size)]
                for i in range(size)
            ]
        )
        scaled = []
        for i in range(size):
            value = (pivots[i][0] * rows[0] + pivots[i][1] * rows[1]) + (
                pivots[i][2] * rows[2] + pivots[i][3] * rows[3]
            )
            for j in range(size):
                value = jnp.where(lane == k + j, pivots[i][j], value)
            scaled.append(value)
        inside = (lane >= k) & (lane < k + size)
        rest = []
        for t, tile in enumerate(tiles):
            value = jnp.where(inside, 0.0, tile)
            for j in range(size):
                value = value - columns[j][t] * scaled[j]
            rest.append(value)
        for i in range(size):
            rest[home] = jnp.where(row == start + i, scaled[i], rest[home])
        tiles = rest
    return jnp.concatenate(tiles, 0)


def solve(own, west, east, out):
    row = lax.broadcasted_iota(jnp.int32, (SYSTEM_ROWS, LANES), 0)
    diagonal = row == lane_index((SYSTEM_ROWS, LANES))
    identity = jnp.where(diagonal & (row < ENSEMBLE), 1.0, 0.0)
    system = identity + own[...] + 0.5 * (west[...] + east[...])
    solved = inverse([system[8 * t : 8 * t + 8] for t in range(SYSTEM_ROWS // 8)])
    out[...] = 0.5 * (identity + solved)[:ENSEMBLE] - solved[ENSEMBLE : ENSEMBLE + 1]


def update(weights, received, out):
    left = weights[:, :ENSEMBLE]
    for r in range(ROWS):
        halves = [
            received[:, first : first + MEMBERS, :].reshape(ENSEMBLE, LANES)
            for first in (r * MEMBERS, HALF_ROWS + r * MEMBERS)
        ]
        result = jnp.dot(
            left, jnp.concatenate(halves, 1), precision=HIGHEST,
            preferred_element_type=jnp.float32,
        )
        for m in range(ENSEMBLE // MEMBERS):
            rows = result[m * MEMBERS : (m + 1) * MEMBERS]
            out[m, pl.ds(r, MEMBERS, stride=ROWS), :] = rows[:, :LANES]
            out[m, pl.ds(HALF_ROWS + r, MEMBERS, stride=ROWS), :] = rows[:, LANES:]


def unpack(planes, out, left):
    copies = []
    for q in range(PLANES):
        for half in range(2):
            copies.append(
                pltpu.make_async_copy(
                    planes.at[q, half],
                    out.at[:, q, :, half * LANES : (half + 1) * LANES],
                    left.at[q, half],
                )
            )
    for copy in copies:
        copy.start()
    for copy in copies:
        copy.wait()


def vmem():
    return pl.BlockSpec(memory_space=pltpu.VMEM)


def hbm():
    return pl.BlockSpec(memory_space=pltpu.HBM)


def kernel(body, operands, *shapes, scalars=(), fetched=(), scratch=(), out_spec=vmem):
    fetched = [pltpu.with_memory_space_constraint(x, pltpu.HBM) for x in fetched]
    shapes = [s if hasattr(s, "dtype") else jax.ShapeDtypeStruct(s, jnp.float32) for s in shapes]
    return pl.pallas_call(
        body,
        out_shape=shapes,
        in_specs=[vmem()] * len(operands)
        + [pl.BlockSpec(memory_space=pltpu.SMEM)] * len(scalars)
        + [hbm()] * len(fetched),
        out_specs=[out_spec() for _ in shapes],
        scratch_shapes=scratch,
        compiler_params=PARAMS,
        name=body.__name__,
    )(*operands, *scalars, *fetched)


def shifted(value, step):
    count = lax.axis_size("tile")
    return lax.ppermute(value, "tile", [(i, (i + step) % count) for i in range(count)])


def exchanged(value):
    return lax.all_to_all(value, "mem", split_axis=0, concat_axis=0, tiled=True)


def local(
    member_tracer_state, diffusivity, velocity, wet_mask, obs_cell, obs_count, obs_value, obs_error
):
    first, last, *blocks = kernel(
        pack_edges,
        (),
        (ROWS, COLUMNS),
        (ROWS, COLUMNS),
        member_tracer_state.shape,
        (2 * LEVELS, ROWS, COLUMNS),
        jax.ShapeDtypeStruct((ROWS, COLUMNS), jnp.int32),
        fetched=(member_tracer_state, diffusivity, velocity, wet_mask),
        scratch=[pltpu.SemaphoreType.DMA((5,))],
    )
    halos = (shifted(last, 1), shifted(first, -1))
    observed, slots = kernel(
        observe,
        (*blocks, *halos),
        (PLANES, MEMBERS, SLOTS),
        (8, SLOTS),
        scalars=(obs_count,),
        fetched=[x.reshape(1, SLOTS) for x in (obs_cell, obs_value, obs_error)],
        scratch=[
            pltpu.VMEM((1, SLOTS), jnp.int32),
            pltpu.VMEM((1, SLOTS), jnp.float32),
            pltpu.VMEM((1, SLOTS), jnp.float32),
            pltpu.SemaphoreType.DMA((3,)),
        ],
    )
    observed = exchanged(observed)
    (chunks,) = kernel(transport, (*blocks, *halos), (PLANES, CELL_ROWS, LANES))
    (share,) = kernel(block_system, (observed, slots), (SYSTEM_ROWS, LANES))
    share, chunks = lax.optimization_barrier((share, chunks))
    received = exchanged(chunks)
    shares = (share, shifted(share, 1), shifted(share, -1))
    (weights,) = kernel(solve, shares, (ENSEMBLE, LANES))
    (updated,) = kernel(update, (weights, received), (PLANES, CELL_ROWS, LANES))
    back = exchanged(updated)
    (analysis,) = kernel(
        unpack,
        (back.reshape(PLANES, 2, MEMBERS, ROWS, LANES),),
        member_tracer_state.shape,
        scratch=[pltpu.SemaphoreType.DMA((PLANES, 2))],
        out_spec=hbm,
    )
    return analysis


def solution(mesh):
    in_specs = (
        P("mem", None, None, "tile"),
        P(None, None, "tile"),
        P(None, None, "tile"),
        P(None, "tile"),
        P("tile"),
        P("tile"),
        P("tile"),
        P("tile"),
    )
    out_specs = P("mem", None, None, "tile")
    return jax.shard_map(local, mesh=mesh, in_specs=in_specs, out_specs=out_specs, check_vma=False)
```

```python
import jax
import jax.numpy as jnp
from jax import lax
from jax.experimental import pallas as pl
from jax.experimental.pallas import tpu as pltpu
from jax.sharding import PartitionSpec as P

LEVELS = 4
PLANES = 8
MEMBERS = 8
PARTS = 4
ENSEMBLE = 64
ROWS = 16
COLUMNS = 256
SLOTS = 128
LANES = 128
HALF_ROWS = ROWS * MEMBERS
CELL_ROWS = 2 * HALF_ROWS
CHUNK_ROWS = CELL_ROWS + 3 * MEMBERS
SYSTEM_ROWS = ENSEMBLE + 8
TRACER_LANES, STATIC_LANES = slice(0, LANES), slice(LANES, 2 * LANES)
HIGHEST = lax.Precision.HIGHEST
PARAMS = pltpu.CompilerParams(vmem_limit_bytes=32 * 1024 * 1024)


def lane_index(shape):
    return lax.broadcasted_iota(jnp.int32, shape, 1)


def pack_edges(
    state, diffusivity, velocity, wet, cell, value, error, off_chip, on_chip, own_state, own_statics,
    own_wet, own_cell, own_value, own_error, arrived
):
    odd = lax.axis_index("tile") % 2 == 1

    def hand_out(lanes, first, last):
        on_chip[:, lanes] = jnp.where(odd, first, last)
        off_chip[:, lanes] = jnp.where(odd, last, first)

    copies = []
    for part in range(PARTS):
        rows = slice(part * MEMBERS // PARTS, (part + 1) * MEMBERS // PARTS)
        copies.append((state.at[rows], own_state.at[rows]))
    copies += [
        (diffusivity, own_statics.at[:LEVELS]),
        (velocity, own_statics.at[LEVELS:]),
        (wet, own_wet),
        (cell, own_cell),
        (value, own_value),
        (error, own_error),
    ]
    copies = [
        pltpu.make_async_copy(source, target, arrived.at[i])
        for i, (source, target) in enumerate(copies)
    ]
    for copy in copies:
        copy.start()
    pair = lane_index((ROWS, LANES)) >> 1

    def put(low, high, index, kept):
        first_kept, last_kept = kept
        first_kept = jnp.where(pair == index, pltpu.roll(low, 2 * index, 1), first_kept)
        last_kept = jnp.where(
            pair == index, pltpu.roll(high, (2 * index + 2) % LANES, 1), last_kept
        )
        return first_kept, last_kept

    def member(e, kept):
        for q in range(PLANES):
            low, high = own_state[e, q, :, :LANES], own_state[e, q, :, LANES:]
            kept = put(low, high, e * PLANES + q, kept)
        return kept

    zeros = jnp.zeros((ROWS, LANES), jnp.float32)
    kept = (zeros, zeros)
    for part in range(PARTS):
        copies[part].wait()
        kept = lax.fori_loop(part * MEMBERS // PARTS, (part + 1) * MEMBERS // PARTS, member, kept)
    hand_out(TRACER_LANES, *kept)
    for copy in copies[PARTS:]:
        copy.wait()
    kept = (zeros, zeros)
    for i in range(2 * LEVELS):
        kept = put(own_statics[i, :, :LANES], own_statics[i, :, LANES:], i, kept)
    flags = own_wet[...].astype(jnp.float32)
    kept = put(flags[:, :LANES], flags[:, LANES:], 2 * LEVELS, kept)
    hand_out(STATIC_LANES, *kept)


def halos(off_chip, on_chip):
    odd = lax.axis_index("tile") % 2 == 1
    one, other = on_chip[...], off_chip[...]
    return jnp.where(odd, one, other), jnp.where(odd, other, one)


def from_west(tiles):
    lane = lane_index((ROWS, LANES))
    turned = [pltpu.roll(tile, 1, 1) for tile in tiles]
    return [jnp.where(lane == 0, turned[i - 1], turned[i]) for i in range(3)]


def from_east(tiles):
    lane = lane_index((ROWS, LANES))
    turned = [pltpu.roll(tile, LANES - 1, 1) for tile in tiles]
    return [jnp.where(lane == LANES - 1, turned[(i + 1) % 3], turned[i]) for i in range(3)]


def halo_tile(west, east, index):
    lane = lane_index((ROWS, LANES))
    east = pltpu.roll(east, (LANES - 2 * index) % LANES, 1)
    west = pltpu.roll(west, LANES - 2 - 2 * index, 1)
    return jnp.where(lane < 2, east, jnp.where(lane >= LANES - 2, west, 0.0))


def widened(block, west_halo, east_halo, lanes, index):
    halo = halo_tile(west_halo[:, lanes], east_halo[:, lanes], index)
    return [block[:, :LANES], block[:, LANES:], halo]


def stepper(level, statics, wet, west_halo, east_halo):
    row = lax.broadcasted_iota(jnp.int32, (ROWS, LANES), 0)
    halos = (west_halo, east_halo, STATIC_LANES)
    ocean = widened(wet[...].astype(jnp.float32), *halos, 2 * LEVELS)
    diffuse = widened(statics[level], *halos, level)
    speed = widened(statics[LEVELS + level], *halos, LEVELS + level)
    ocean_west, diffuse_west, speed_west = map(from_west, (ocean, diffuse, speed))
    face_west, face_east, north = [], [], []
    for i in range(3):
        face = ocean_west[i] * ocean[i]
        a = 0.5 * (speed_west[i] + speed[i])
        k = 0.5 * (diffuse_west[i] + diffuse[i])
        face_west.append(face * (jnp.maximum(a, 0.0) + k))
        face_east.append(face * (jnp.minimum(a, 0.0) - k))
        k = 0.5 * (diffuse[i] + pltpu.roll(diffuse[i], ROWS - 1, 0))
        both = ocean[i] * pltpu.roll(ocean[i], ROWS - 1, 0)
        north.append(jnp.where(row < ROWS - 1, both * k, 0.0))
    next_west, next_east = from_east(face_west), from_east(face_east)
    above = [pltpu.roll(x, 1, 0) for x in north]
    centre = [
        1.0 + (face_east[i] - next_west[i] - above[i] - north[i]) * ocean[i] for i in range(3)
    ]

    def advance(tiles, count):
        west, east = from_west(tiles), from_east(tiles)
        return [
            centre[i] * tiles[i]
            + face_west[i] * west[i]
            - next_east[i] * east[i]
            + above[i] * pltpu.roll(tiles[i], 1, 0)
            + north[i] * pltpu.roll(tiles[i], ROWS - 1, 0)
            for i in range(count)
        ]

    return lambda tiles: advance(advance(tiles, 3), 2)


def transport(state, statics, wet, off_chip, on_chip, chunks):
    west_halo, east_halo = halos(off_chip, on_chip)

    def level_step(level, carry):
        steps = stepper(level, statics, wet, west_halo, east_halo)

        def member_step(e, carry):
            for tracer in range(2):
                q = tracer * LEVELS + level
                done = steps(
                    widened(state[e, q], west_halo, east_halo, TRACER_LANES, e * PLANES + q)
                )
                for half in range(2):
                    rows = pl.ds(half * HALF_ROWS + e, ROWS, stride=MEMBERS)
                    chunks[q, rows, :] = done[half]
            return carry

        return lax.fori_loop(0, MEMBERS, member_step, carry, unroll=4)

    lax.fori_loop(0, LEVELS, level_step, 0)


def observe(state, statics, wet, off_chip, on_chip, cell, value, error, count, out):
    west_halo, east_halo = halos(off_chip, on_chip)
    steps = stepper(0, statics, wet, west_halo, east_halo)
    surface = []
    for e in range(MEMBERS):
        done = steps(widened(state[e, 0], west_halo, east_halo, TRACER_LANES, e * PLANES))
        surface.append(jnp.concatenate(done, 1))
    in_use = (lane_index((1, SLOTS)) < count[0]).astype(jnp.float32)
    scale = 1.0 / ((ENSEMBLE - 1) * error[...])
    unused = jnp.zeros((5, SLOTS), jnp.float32)
    out[MEMBERS:, :] = jnp.concatenate([in_use, value[...], scale, unused], 0)
    cell = cell[...]
    column = lax.broadcasted_iota(jnp.int32, (COLUMNS, SLOTS), 0)
    pick = (column == (cell & (COLUMNS - 1))).astype(jnp.float32)
    near = jnp.dot(
        jnp.concatenate(surface, 0), pick, precision=HIGHEST, preferred_element_type=jnp.float32
    )
    layer = lax.broadcasted_iota(jnp.int32, (ROWS, SLOTS), 0)
    chosen = layer == (cell >> 8)
    for e in range(MEMBERS):
        kept = jnp.where(chosen, near[e * ROWS : (e + 1) * ROWS], 0.0)
        out[e : e + 1, :] = jnp.sum(kept, 0, keepdims=True)


def attach(chunks, own, off_chip, on_chip, out):
    for i, block in enumerate((own, off_chip, on_chip)):
        values = block[:MEMBERS]
        for q in range(PLANES):
            out[q, pl.ds(CELL_ROWS + i * MEMBERS, MEMBERS), :] = values


def gram(received, blocks):
    first = lax.broadcasted_iota(jnp.int32, (8, SLOTS), 0) == 0
    unused = jnp.zeros((LANES - ENSEMBLE, SLOTS), jnp.float32)
    left, right = [], []
    for i, (block, locality) in enumerate(zip(blocks, (1.0, 0.5, 0.5))):
        rows = pl.ds(CELL_ROWS + i * MEMBERS, MEMBERS)
        members = received[:, rows, :].reshape(ENSEMBLE, SLOTS)
        in_use, value, scale = (block[MEMBERS + j : MEMBERS + j + 1] for j in range(3))
        mean = jnp.sum(members, 0, keepdims=True) / ENSEMBLE
        anomaly = (members - mean) * in_use
        innovation = (value - mean) * in_use
        left.append(jnp.concatenate([anomaly, jnp.where(first, innovation, 0.0)], 0))
        right.append(jnp.concatenate([anomaly * (scale * locality), unused], 0))
    return lax.dot_general(
        jnp.concatenate(left, 1), jnp.concatenate(right, 1), (((1,), (1,)), ((), ())),
        precision=HIGHEST, preferred_element_type=jnp.float32,
    )


def symmetric_inverse(a, b, c):
    scale = 1.0 / (a * c - b * b)
    return c * scale, -b * scale, a * scale


def pivot_inverse(e):
    a0, a1, a2 = symmetric_inverse(e[0][0], e[0][1], e[1][1])
    b00, b01, b10, b11 = e[0][2], e[0][3], e[1][2], e[1][3]
    f00, f01 = a0 * b00 + a1 * b10, a0 * b01 + a1 * b11
    f10, f11 = a1 * b00 + a2 * b10, a1 * b01 + a2 * b11
    s0, s1, s2 = symmetric_inverse(
        e[2][2] - (b00 * f00 + b10 * f10),
        e[2][3] - (b00 * f01 + b10 * f11),
        e[3][3] - (b01 * f01 + b11 * f11),
    )
    t00, t01 = f00 * s0 + f01 * s1, f00 * s1 + f01 * s2
    t10, t11 = f10 * s0 + f11 * s1, f10 * s1 + f11 * s2
    x01 = a1 + t00 * f10 + t01 * f11
    return [
        [a0 + t00 * f00 + t01 * f01, x01, -t00, -t01],
        [x01, a2 + t10 * f10 + t11 * f11, -t10, -t11],
        [-t00, -t10, s0, s1],
        [-t01, -t11, s1, s2],
    ]


def inverse(tiles):
    row = lax.broadcasted_iota(jnp.int32, (8, LANES), 0)
    lane = lane_index((8, LANES))
    size = 4

    def everywhere(block):
        return jnp.broadcast_to(block, (8, LANES))

    for k in range(0, ENSEMBLE, size):
        home, start = k // 8, k % 8
        columns = [[everywhere(tile[:, k + j : k + j + 1]) for tile in tiles] for j in range(size)]
        rows = [everywhere(tiles[home][start + i : start + i + 1]) for i in range(size)]
        pivots = pivot_inverse(
            [
                [everywhere(columns[j][home][start + i : start + i + 1]) for j in range(size)]
                for i in range(size)
            ]
        )
        scaled = []
        for i in range(size):
            value = (pivots[i][0] * rows[0] + pivots[i][1] * rows[1]) + (
                pivots[i][2] * rows[2] + pivots[i][3] * rows[3]
            )
            for j in range(size):
                value = jnp.where(lane == k + j, pivots[i][j], value)
            scaled.append(value)
        inside = (lane >= k) & (lane < k + size)
        rest = []
        for t, tile in enumerate(tiles):
            value = jnp.where(inside, 0.0, tile)
            for j in range(size):
                value = value - columns[j][t] * scaled[j]
            rest.append(value)
        for i in range(size):
            rest[home] = jnp.where(row == start + i, scaled[i], rest[home])
        tiles = rest
    return jnp.concatenate(tiles, 0)


def analyse(received, own, off_chip, on_chip, out):
    row = lax.broadcasted_iota(jnp.int32, (SYSTEM_ROWS, LANES), 0)
    diagonal = row == lane_index((SYSTEM_ROWS, LANES))
    identity = jnp.where(diagonal & (row < ENSEMBLE), 1.0, 0.0)
    system = identity + gram(received, (own, off_chip, on_chip))
    solved = inverse([system[8 * t : 8 * t + 8] for t in range(SYSTEM_ROWS // 8)])
    weights = 0.5 * (identity + solved)[:ENSEMBLE] - solved[ENSEMBLE : ENSEMBLE + 1]
    weights = weights[:, :ENSEMBLE]
    for r in range(ROWS):
        halves = [
            received[:, first : first + MEMBERS, :].reshape(ENSEMBLE, LANES)
            for first in (r * MEMBERS, HALF_ROWS + r * MEMBERS)
        ]
        result = jnp.dot(
            weights, jnp.concatenate(halves, 1), precision=HIGHEST,
            preferred_element_type=jnp.float32,
        )
        for m in range(ENSEMBLE // MEMBERS):
            rows = result[m * MEMBERS : (m + 1) * MEMBERS]
            out[m, pl.ds(r, MEMBERS, stride=ROWS), :] = rows[:, :LANES]
            out[m, pl.ds(HALF_ROWS + r, MEMBERS, stride=ROWS), :] = rows[:, LANES:]


def unpack(planes, out, left):
    copies = []
    for q in range(PLANES):
        for half in range(2):
            copies.append(
                pltpu.make_async_copy(
                    planes.at[q, half],
                    out.at[:, q, :, half * LANES : (half + 1) * LANES],
                    left.at[q, half],
                )
            )
    for copy in copies:
        copy.start()
    for copy in copies:
        copy.wait()


def vmem():
    return pl.BlockSpec(memory_space=pltpu.VMEM)


def hbm():
    return pl.BlockSpec(memory_space=pltpu.HBM)


def kernel(
    body, operands, *shapes, scalars=(), fetched=(), scratch=(), out_spec=vmem, aliases={}
):
    fetched = [pltpu.with_memory_space_constraint(x, pltpu.HBM) for x in fetched]
    shapes = [s if hasattr(s, "dtype") else jax.ShapeDtypeStruct(s, jnp.float32) for s in shapes]
    return pl.pallas_call(
        body,
        out_shape=shapes,
        in_specs=[vmem()] * len(operands)
        + [pl.BlockSpec(memory_space=pltpu.SMEM)] * len(scalars)
        + [hbm()] * len(fetched),
        out_specs=[out_spec() for _ in shapes],
        scratch_shapes=scratch,
        input_output_aliases=aliases,
        compiler_params=PARAMS,
        name=body.__name__,
    )(*operands, *scalars, *fetched)


def swapped(value, start):
    count = lax.axis_size("tile")
    pairs = [((i + start) % count, (i + 1 + start) % count) for i in range(0, count, 2)]
    return lax.ppermute(value, "tile", pairs + [(b, a) for a, b in pairs])


def both_neighbours(off_chip, on_chip):
    far = swapped(off_chip, 1)
    return far, swapped(on_chip, 0)


def exchanged(value):
    return lax.all_to_all(value, "mem", split_axis=0, concat_axis=0, tiled=True)


def local(
    member_tracer_state, diffusivity, velocity, wet_mask, obs_cell, obs_count, obs_value, obs_error
):
    slot_rows = [x.reshape(1, SLOTS) for x in (obs_cell, obs_value, obs_error)]
    off_chip, on_chip, *blocks, cell, value, error = kernel(
        pack_edges,
        (),
        (ROWS, COLUMNS),
        (ROWS, COLUMNS),
        member_tracer_state.shape,
        (2 * LEVELS, ROWS, COLUMNS),
        jax.ShapeDtypeStruct((ROWS, COLUMNS), jnp.int32),
        jax.ShapeDtypeStruct((1, SLOTS), jnp.int32),
        (1, SLOTS),
        (1, SLOTS),
        fetched=(member_tracer_state, diffusivity, velocity, wet_mask, *slot_rows),
        scratch=[pltpu.SemaphoreType.DMA((PARTS + 6,))],
    )
    edges = both_neighbours(off_chip, on_chip)
    (own,) = kernel(
        observe, (*blocks, *edges, cell, value, error), (2 * MEMBERS, SLOTS), scalars=(obs_count,)
    )
    near = (own, *both_neighbours(own, own))
    (chunks,) = kernel(transport, (*blocks, *edges), (PLANES, CHUNK_ROWS, LANES))
    (chunks,) = kernel(attach, (chunks, *near), chunks.shape, aliases={0: 0})
    received = exchanged(chunks)
    (updated,) = kernel(analyse, (received, *near), (PLANES, CELL_ROWS, LANES))
    back = exchanged(updated)
    (analysis,) = kernel(
        unpack,
        (back.reshape(PLANES, 2, MEMBERS, ROWS, LANES),),
        member_tracer_state.shape,
        scratch=[pltpu.SemaphoreType.DMA((PLANES, 2))],
        out_spec=hbm,
    )
    return analysis


def solution(mesh):
    in_specs = (
        P("mem", None, None, "tile"),
        P(None, None, "tile"),
        P(None, None, "tile"),
        P(None, "tile"),
        P("tile"),
        P("tile"),
        P("tile"),
        P("tile"),
    )
    out_specs = P("mem", None, None, "tile")
    return jax.shard_map(local, mesh=mesh, in_specs=in_specs, out_specs=out_specs, check_vma=False)
```

```python
import jax
import jax.numpy as jnp
from jax import lax
from jax.experimental import pallas as pl
from jax.experimental.pallas import tpu as pltpu
from jax.sharding import PartitionSpec as P

LEVELS = 4
PLANES = 8
MEMBERS = 8
PARTS = 4
ENSEMBLE = 64
ROWS = 16
COLUMNS = 256
SLOTS = 128
LANES = 128
HALF_ROWS = ROWS * MEMBERS
CELL_ROWS = 2 * HALF_ROWS
CHUNK_ROWS = CELL_ROWS + 3 * MEMBERS
SYSTEM_ROWS = ENSEMBLE + 8
TRACER_LANES, STATIC_LANES = slice(0, LANES), slice(LANES, 2 * LANES)
HIGHEST = lax.Precision.HIGHEST
PARAMS = pltpu.CompilerParams(vmem_limit_bytes=32 * 1024 * 1024)


def lane_index(shape):
    return lax.broadcasted_iota(jnp.int32, shape, 1)


def pack_edges(
    state, diffusivity, velocity, wet, cell, value, error, off_chip, on_chip, own_state, own_statics,
    own_wet, own_cell, own_value, own_error, arrived
):
    odd = lax.axis_index("tile") % 2 == 1

    def hand_out(lanes, first, last):
        on_chip[:, lanes] = jnp.where(odd, first, last)
        off_chip[:, lanes] = jnp.where(odd, last, first)

    copies = []
    for part in range(PARTS):
        rows = slice(part * MEMBERS // PARTS, (part + 1) * MEMBERS // PARTS)
        copies.append((state.at[rows], own_state.at[rows]))
    copies += [
        (diffusivity, own_statics.at[:LEVELS]),
        (velocity, own_statics.at[LEVELS:]),
        (wet, own_wet),
        (cell, own_cell),
        (value, own_value),
        (error, own_error),
    ]
    copies = [
        pltpu.make_async_copy(source, target, arrived.at[i])
        for i, (source, target) in enumerate(copies)
    ]
    for copy in copies:
        copy.start()
    pair = lane_index((ROWS, LANES)) >> 1

    def put(low, high, index, kept):
        first_kept, last_kept = kept
        first_kept = jnp.where(pair == index, pltpu.roll(low, 2 * index, 1), first_kept)
        last_kept = jnp.where(
            pair == index, pltpu.roll(high, (2 * index + 2) % LANES, 1), last_kept
        )
        return first_kept, last_kept

    def member(e, kept):
        for q in range(PLANES):
            low, high = own_state[e, q, :, :LANES], own_state[e, q, :, LANES:]
            kept = put(low, high, e * PLANES + q, kept)
        return kept

    zeros = jnp.zeros((ROWS, LANES), jnp.float32)
    kept = (zeros, zeros)
    for part in range(PARTS):
        copies[part].wait()
        rows = range(part * MEMBERS // PARTS, (part + 1) * MEMBERS // PARTS)
        for e in rows:
            kept = member(e, kept)
    hand_out(TRACER_LANES, *kept)
    for copy in copies[PARTS:]:
        copy.wait()
    kept = (zeros, zeros)
    for i in range(2 * LEVELS):
        kept = put(own_statics[i, :, :LANES], own_statics[i, :, LANES:], i, kept)
    flags = own_wet[...].astype(jnp.float32)
    kept = put(flags[:, :LANES], flags[:, LANES:], 2 * LEVELS, kept)
    hand_out(STATIC_LANES, *kept)


def sides(sent_off, sent_on, off_chip, on_chip, lanes):
    odd_block = lax.axis_index("tile") % 2 == 1
    off, on = off_chip[:, lanes], on_chip[:, lanes]
    west, east = jnp.where(odd_block, on, off), jnp.where(odd_block, off, on)
    off, on = sent_off[:, lanes], sent_on[:, lanes]
    own_first, own_last = jnp.where(odd_block, on, off), jnp.where(odd_block, off, on)
    odd = lane_index((ROWS, LANES)) % 2 == 1
    inner = jnp.where(odd, pltpu.roll(own_first, 1, 1), pltpu.roll(own_last, LANES - 1, 1))
    outer = jnp.where(odd, pltpu.roll(west, 1, 1), pltpu.roll(east, LANES - 1, 1))
    return inner, jnp.where(odd, west, east), outer


def repeated(block, start, width):
    lane = lane_index((ROWS, LANES))
    if start:
        block = pltpu.roll(block, LANES - start, 1)
    block = jnp.where(lane < width, block, 0.0)
    while width < LANES:
        block = block + pltpu.roll(block, width, 1)
        width *= 2
    return block


def face(wet, speed, diffuse):
    a = 0.5 * (speed[0] + speed[1])
    k = 0.5 * (diffuse[0] + diffuse[1])
    ocean = wet[0] * wet[1]
    return ocean * (jnp.maximum(a, 0.0) + k), ocean * (jnp.minimum(a, 0.0) - k)


def rows_between(wet, diffuse):
    row = lax.broadcasted_iota(jnp.int32, (ROWS, LANES), 0)
    both = wet * pltpu.roll(wet, ROWS - 1, 0)
    k = 0.5 * (diffuse + pltpu.roll(diffuse, ROWS - 1, 0))
    north = jnp.where(row < ROWS - 1, both * k, 0.0)
    return pltpu.roll(north, 1, 0), north


def five_point(weights, cell, west, east):
    centre, to_west, to_east, above, north = weights
    return (
        centre * cell
        + to_west * west
        + to_east * east
        + above * pltpu.roll(cell, 1, 0)
        + north * pltpu.roll(cell, ROWS - 1, 0)
    )


def border(edges):
    odd = lane_index((ROWS, LANES)) % 2 == 1
    inner, cell, outer = sides(*edges, TRACER_LANES)
    statics = sides(*edges, STATIC_LANES)
    diffuse = [repeated(x, 0, 2 * LEVELS) for x in statics]
    speed = [repeated(x, 2 * LEVELS, 2 * LEVELS) for x in statics]
    wet = [repeated(x, 4 * LEVELS, 2) for x in statics]
    in_west, in_east = face(wet[:2], speed[:2], diffuse[:2])
    out_west, out_east = face(wet[1:], speed[1:], diffuse[1:])
    above, north = rows_between(wet[1], diffuse[1])
    zonal = jnp.where(odd, out_east - in_west, in_east - out_west)
    centre = 1.0 + (zonal - above - north) * wet[1]
    to_inner = jnp.where(odd, -in_east, in_west)
    to_outer = jnp.where(odd, out_west, -out_east)
    stepped = five_point((centre, to_inner, to_outer, above, north), cell, inner, outer)
    return cell, stepped


def neighbours(tiles, halo):
    return bordered(
        [pltpu.roll(tile, 1, 1) for tile in tiles],
        [pltpu.roll(tile, LANES - 1, 1) for tile in tiles],
        halo,
    )


def bordered(west, east, halo):
    lane = lane_index((ROWS, LANES))
    first, last = lane == 0, lane == LANES - 1
    west = [jnp.where(first, halo, west[0]), jnp.where(first, west[0], west[1])]
    return west, [jnp.where(last, east[1], east[0]), jnp.where(last, halo, east[1])]


def turns():
    row = lax.broadcasted_iota(jnp.int32, (2 * LANES, 2 * LANES), 0)
    column = lax.broadcasted_iota(jnp.int32, (2 * LANES, 2 * LANES), 1)
    source = jnp.where(column < LANES, column + LANES - 1, column + 1) % LANES
    return (row % LANES == source).astype(jnp.bfloat16)


def split(block):
    high = block.astype(jnp.bfloat16)
    return high, (block - high.astype(jnp.float32)).astype(jnp.bfloat16)


def aligned(block, index):
    return pltpu.roll(block, LANES - 1 - 2 * index, 1)


def halved(block):
    return [block[:, :LANES], block[:, LANES:]]


def stepper(level, statics, wet, edges):
    cells = sides(*edges, STATIC_LANES)[1]
    ocean = halved(wet[...].astype(jnp.float32))
    diffuse, speed = halved(statics[level]), halved(statics[LEVELS + level])
    (wet_west, wet_east), (diffuse_west, diffuse_east), (speed_west, speed_east) = (
        neighbours(tiles, aligned(cells, index))
        for tiles, index in ((ocean, 2 * LEVELS), (diffuse, level), (speed, LEVELS + level))
    )
    weights = []
    for i in range(2):
        west = face((wet_west[i], ocean[i]), (speed_west[i], speed[i]), (diffuse_west[i], diffuse[i]))
        east = face((ocean[i], wet_east[i]), (speed[i], speed_east[i]), (diffuse[i], diffuse_east[i]))
        above, north = rows_between(ocean[i], diffuse[i])
        centre = 1.0 + (west[1] - east[0] - above - north) * ocean[i]
        weights.append((centre, west[0], -east[1], above, north))

    return weights


def two_steps(weights, turn, planes, borders):
    count = len(planes)
    for halos in borders:
        stacked = jnp.concatenate([tiles[half] for half in range(2) for tiles in planes], 0)
        moved = jnp.dot(
            jnp.concatenate(split(stacked), 1), turn, preferred_element_type=jnp.float32
        )
        stepped = []
        for i in range(count):
            turned = [
                halved(moved[(half * count + i) * ROWS : (half * count + i + 1) * ROWS])
                for half in range(2)
            ]
            west, east = bordered(*zip(*turned), halos[i])
            stepped.append(
                [five_point(weights[h], planes[i][h], west[h], east[h]) for h in range(2)]
            )
        planes = stepped
    return planes


def transport(state, statics, wet, sent_off, sent_on, off_chip, on_chip, sides_of, chunks):
    edges = (sent_off, sent_on, off_chip, on_chip)
    borders = (sides_of[:ROWS], sides_of[ROWS:])
    turn = turns()

    def level_step(level, carry):
        weights = stepper(level, statics, wet, edges)
        where = [(e, t * LEVELS + level) for e in range(MEMBERS) for t in range(2)]
        planes = [halved(state[e, q]) for e, q in where]
        halos = [[aligned(block, e * PLANES + q) for e, q in where] for block in borders]
        for (e, q), done in zip(where, two_steps(weights, turn, planes, halos)):
            for half in range(2):
                rows = pl.ds(half * HALF_ROWS + e, ROWS, stride=MEMBERS)
                chunks[q, rows, :] = done[half]
        return carry

    lax.fori_loop(0, LEVELS, level_step, 0)


def observe(
    state, statics, wet, sent_off, sent_on, off_chip, on_chip, cell, value, error, count, out, sides_of
):
    edges = (sent_off, sent_on, off_chip, on_chip)
    borders = border(edges)
    sides_of[:ROWS], sides_of[ROWS:] = borders
    weights = stepper(0, statics, wet, edges)
    planes = [halved(state[e, 0]) for e in range(MEMBERS)]
    halos = [[aligned(block, e * PLANES) for e in range(MEMBERS)] for block in borders]
    surface = [jnp.concatenate(x, 1) for x in two_steps(weights, turns(), planes, halos)]
    in_use = (lane_index((1, SLOTS)) < count[0]).astype(jnp.float32)
    scale = 1.0 / ((ENSEMBLE - 1) * error[...])
    unused = jnp.zeros((5, SLOTS), jnp.float32)
    out[MEMBERS:, :] = jnp.concatenate([in_use, value[...], scale, unused], 0)
    cell = cell[...]
    column = lax.broadcasted_iota(jnp.int32, (COLUMNS, SLOTS), 0)
    pick = (column == (cell & (COLUMNS - 1))).astype(jnp.float32)
    near = jnp.dot(
        jnp.concatenate(surface, 0), pick, precision=HIGHEST, preferred_element_type=jnp.float32
    )
    layer = lax.broadcasted_iota(jnp.int32, (ROWS, SLOTS), 0)
    chosen = layer == (cell >> 8)
    for e in range(MEMBERS):
        kept = jnp.where(chosen, near[e * ROWS : (e + 1) * ROWS], 0.0)
        out[e : e + 1, :] = jnp.sum(kept, 0, keepdims=True)


def attach(chunks, own, off_chip, on_chip, out):
    for i, block in enumerate((own, off_chip, on_chip)):
        values = block[:MEMBERS]
        for q in range(PLANES):
            out[q, pl.ds(CELL_ROWS + i * MEMBERS, MEMBERS), :] = values


def gram(received, blocks):
    first = lax.broadcasted_iota(jnp.int32, (8, SLOTS), 0) == 0
    unused = jnp.zeros((LANES - ENSEMBLE, SLOTS), jnp.float32)
    left, right = [], []
    for i, (block, locality) in enumerate(zip(blocks, (1.0, 0.5, 0.5))):
        rows = pl.ds(CELL_ROWS + i * MEMBERS, MEMBERS)
        members = received[:, rows, :].reshape(ENSEMBLE, SLOTS)
        in_use, value, scale = (block[MEMBERS + j : MEMBERS + j + 1] for j in range(3))
        mean = jnp.sum(members, 0, keepdims=True) / ENSEMBLE
        anomaly = (members - mean) * in_use
        innovation = (value - mean) * in_use
        left.append(jnp.concatenate([anomaly, jnp.where(first, innovation, 0.0)], 0))
        right.append(jnp.concatenate([anomaly * (scale * locality), unused], 0))
    return lax.dot_general(
        jnp.concatenate(left, 1), jnp.concatenate(right, 1), (((1,), (1,)), ((), ())),
        precision=HIGHEST, preferred_element_type=jnp.float32,
    )


def symmetric_inverse(a, b, c):
    scale = 1.0 / (a * c - b * b)
    return c * scale, -b * scale, a * scale


def pivot_inverse(e):
    a0, a1, a2 = symmetric_inverse(e[0][0], e[0][1], e[1][1])
    b00, b01, b10, b11 = e[0][2], e[0][3], e[1][2], e[1][3]
    f00, f01 = a0 * b00 + a1 * b10, a0 * b01 + a1 * b11
    f10, f11 = a1 * b00 + a2 * b10, a1 * b01 + a2 * b11
    s0, s1, s2 = symmetric_inverse(
        e[2][2] - (b00 * f00 + b10 * f10),
        e[2][3] - (b00 * f01 + b10 * f11),
        e[3][3] - (b01 * f01 + b11 * f11),
    )
    t00, t01 = f00 * s0 + f01 * s1, f00 * s1 + f01 * s2
    t10, t11 = f10 * s0 + f11 * s1, f10 * s1 + f11 * s2
    x01 = a1 + t00 * f10 + t01 * f11
    return [
        [a0 + t00 * f00 + t01 * f01, x01, -t00, -t01],
        [x01, a2 + t10 * f10 + t11 * f11, -t10, -t11],
        [-t00, -t10, s0, s1],
        [-t01, -t11, s1, s2],
    ]


def inverse(tiles):
    row = lax.broadcasted_iota(jnp.int32, (8, LANES), 0)
    lane = lane_index((8, LANES))
    size = 4

    def everywhere(block):
        return jnp.broadcast_to(block, (8, LANES))

    for k in range(0, ENSEMBLE, size):
        home, start = k // 8, k % 8
        columns = [[everywhere(tile[:, k + j : k + j + 1]) for tile in tiles] for j in range(size)]
        rows = [everywhere(tiles[home][start + i : start + i + 1]) for i in range(size)]
        pivots = pivot_inverse(
            [
                [everywhere(columns[j][home][start + i : start + i + 1]) for j in range(size)]
                for i in range(size)
            ]
        )
        scaled = []
        for i in range(size):
            value = (pivots[i][0] * rows[0] + pivots[i][1] * rows[1]) + (
                pivots[i][2] * rows[2] + pivots[i][3] * rows[3]
            )
            for j in range(size):
                value = jnp.where(lane == k + j, pivots[i][j], value)
            scaled.append(value)
        inside = (lane >= k) & (lane < k + size)
        rest = []
        for t, tile in enumerate(tiles):
            value = jnp.where(inside, 0.0, tile)
            for j in range(size):
                value = value - columns[j][t] * scaled[j]
            rest.append(value)
        for i in range(size):
            rest[home] = jnp.where(row == start + i, scaled[i], rest[home])
        tiles = rest
    return jnp.concatenate(tiles, 0)


def analyse(received, own, off_chip, on_chip, out):
    row = lax.broadcasted_iota(jnp.int32, (SYSTEM_ROWS, LANES), 0)
    diagonal = row == lane_index((SYSTEM_ROWS, LANES))
    identity = jnp.where(diagonal & (row < ENSEMBLE), 1.0, 0.0)
    system = identity + gram(received, (own, off_chip, on_chip))
    solved = inverse([system[8 * t : 8 * t + 8] for t in range(SYSTEM_ROWS // 8)])
    weights = 0.5 * (identity + solved)[:ENSEMBLE] - solved[ENSEMBLE : ENSEMBLE + 1]
    high, low = split(weights[:, :ENSEMBLE])
    weights = jnp.concatenate([high, low, high], 1)
    for r in range(ROWS):
        halves = [
            received[:, first : first + MEMBERS, :].reshape(ENSEMBLE, LANES)
            for first in (r * MEMBERS, HALF_ROWS + r * MEMBERS)
        ]
        high, low = split(jnp.concatenate(halves, 1))
        result = jnp.dot(
            weights, jnp.concatenate([high, high, low], 0), preferred_element_type=jnp.float32
        )
        for m in range(ENSEMBLE // MEMBERS):
            rows = result[m * MEMBERS : (m + 1) * MEMBERS]
            out[m, pl.ds(r, MEMBERS, stride=ROWS), :] = rows[:, :LANES]
            out[m, pl.ds(HALF_ROWS + r, MEMBERS, stride=ROWS), :] = rows[:, LANES:]


def unpack(planes, out, left):
    copies = []
    for q in range(PLANES):
        for half in range(2):
            copies.append(
                pltpu.make_async_copy(
                    planes.at[q, half],
                    out.at[:, q, :, half * LANES : (half + 1) * LANES],
                    left.at[q, half],
                )
            )
    for copy in copies:
        copy.start()
    for copy in copies:
        copy.wait()


def vmem():
    return pl.BlockSpec(memory_space=pltpu.VMEM)


def hbm():
    return pl.BlockSpec(memory_space=pltpu.HBM)


def kernel(
    body, operands, *shapes, scalars=(), fetched=(), scratch=(), out_spec=vmem, aliases={}
):
    fetched = [pltpu.with_memory_space_constraint(x, pltpu.HBM) for x in fetched]
    shapes = [s if hasattr(s, "dtype") else jax.ShapeDtypeStruct(s, jnp.float32) for s in shapes]
    return pl.pallas_call(
        body,
        out_shape=shapes,
        in_specs=[vmem()] * len(operands)
        + [pl.BlockSpec(memory_space=pltpu.SMEM)] * len(scalars)
        + [hbm()] * len(fetched),
        out_specs=[out_spec() for _ in shapes],
        scratch_shapes=scratch,
        input_output_aliases=aliases,
        compiler_params=PARAMS,
        name=body.__name__,
    )(*operands, *scalars, *fetched)


def swapped(value, start):
    count = lax.axis_size("tile")
    pairs = [((i + start) % count, (i + 1 + start) % count) for i in range(0, count, 2)]
    return lax.ppermute(value, "tile", pairs + [(b, a) for a, b in pairs])


def both_neighbours(off_chip, on_chip):
    far = swapped(off_chip, 1)
    return far, swapped(on_chip, 0)


def exchanged(value):
    return lax.all_to_all(value, "mem", split_axis=0, concat_axis=0, tiled=True)


def local(
    member_tracer_state, diffusivity, velocity, wet_mask, obs_cell, obs_count, obs_value, obs_error
):
    slot_rows = [x.reshape(1, SLOTS) for x in (obs_cell, obs_value, obs_error)]
    off_chip, on_chip, *blocks, cell, value, error = kernel(
        pack_edges,
        (),
        (ROWS, COLUMNS),
        (ROWS, COLUMNS),
        member_tracer_state.shape,
        (2 * LEVELS, ROWS, COLUMNS),
        jax.ShapeDtypeStruct((ROWS, COLUMNS), jnp.int32),
        jax.ShapeDtypeStruct((1, SLOTS), jnp.int32),
        (1, SLOTS),
        (1, SLOTS),
        fetched=(member_tracer_state, diffusivity, velocity, wet_mask, *slot_rows),
        scratch=[pltpu.SemaphoreType.DMA((PARTS + 6,))],
    )
    edges = (off_chip, on_chip, *both_neighbours(off_chip, on_chip))
    own, sides_of = kernel(
        observe,
        (*blocks, *edges, cell, value, error),
        (2 * MEMBERS, SLOTS),
        (2 * ROWS, LANES),
        scalars=(obs_count,),
    )
    near = (own, *both_neighbours(own, own))
    (chunks,) = kernel(transport, (*blocks, *edges, sides_of), (PLANES, CHUNK_ROWS, LANES))
    (chunks,) = kernel(attach, (chunks, *near), chunks.shape, aliases={0: 0})
    received = exchanged(chunks)
    (updated,) = kernel(analyse, (received, *near), (PLANES, CELL_ROWS, LANES))
    back = exchanged(updated)
    (analysis,) = kernel(
        unpack,
        (back.reshape(PLANES, 2, MEMBERS, ROWS, LANES),),
        member_tracer_state.shape,
        scratch=[pltpu.SemaphoreType.DMA((PLANES, 2))],
        out_spec=hbm,
    )
    return analysis


def solution(mesh):
    in_specs = (
        P("mem", None, None, "tile"),
        P(None, None, "tile"),
        P(None, None, "tile"),
        P(None, "tile"),
        P("tile"),
        P("tile"),
        P("tile"),
        P("tile"),
    )
    out_specs = P("mem", None, None, "tile")
    return jax.shard_map(local, mesh=mesh, in_specs=in_specs, out_specs=out_specs, check_vma=False)
```

```python
import jax
import jax.numpy as jnp
from jax import lax
from jax.experimental import pallas as pl
from jax.experimental.pallas import tpu as pltpu
from jax.sharding import PartitionSpec as P

LEVELS = 4
PLANES = 8
MEMBERS = 8
PARTS = 4
ENSEMBLE = 64
ROWS = 16
COLUMNS = 256
SLOTS = 128
LANES = 128
HALF_ROWS = ROWS * MEMBERS
CELL_ROWS = 2 * HALF_ROWS
CHUNK_ROWS = CELL_ROWS + 3 * MEMBERS
SYSTEM_ROWS = ENSEMBLE + 8
TRACER_LANES, STATIC_LANES = slice(0, LANES), slice(LANES, 2 * LANES)
HIGHEST = lax.Precision.HIGHEST
PARAMS = pltpu.CompilerParams(vmem_limit_bytes=32 * 1024 * 1024)


def lane_index(shape):
    return lax.broadcasted_iota(jnp.int32, shape, 1)


def pack_edges(
    state, diffusivity, velocity, wet, cell, value, error, off_chip, on_chip, own_state, own_statics,
    own_wet, own_cell, own_value, own_error, arrived
):
    odd = lax.axis_index("tile") % 2 == 1

    def hand_out(lanes, first, last):
        on_chip[:, lanes] = jnp.where(odd, first, last)
        off_chip[:, lanes] = jnp.where(odd, last, first)

    copies = []
    for part in range(PARTS):
        rows = slice(part * MEMBERS // PARTS, (part + 1) * MEMBERS // PARTS)
        copies.append((state.at[rows], own_state.at[rows]))
    copies += [
        (diffusivity, own_statics.at[:LEVELS]),
        (velocity, own_statics.at[LEVELS:]),
        (wet, own_wet),
        (cell, own_cell),
        (value, own_value),
        (error, own_error),
    ]
    copies = [
        pltpu.make_async_copy(source, target, arrived.at[i])
        for i, (source, target) in enumerate(copies)
    ]
    for copy in copies:
        copy.start()
    pair = lane_index((ROWS, LANES)) >> 1

    def put(low, high, index, kept):
        first_kept, last_kept = kept
        first_kept = jnp.where(pair == index, pltpu.roll(low, 2 * index, 1), first_kept)
        last_kept = jnp.where(
            pair == index, pltpu.roll(high, (2 * index + 2) % LANES, 1), last_kept
        )
        return first_kept, last_kept

    def member(e, kept):
        for q in range(PLANES):
            low, high = own_state[e, q, :, :LANES], own_state[e, q, :, LANES:]
            kept = put(low, high, e * PLANES + q, kept)
        return kept

    zeros = jnp.zeros((ROWS, LANES), jnp.float32)
    kept = (zeros, zeros)
    for part in range(PARTS):
        copies[part].wait()
        rows = range(part * MEMBERS // PARTS, (part + 1) * MEMBERS // PARTS)
        for e in rows:
            kept = member(e, kept)
    hand_out(TRACER_LANES, *kept)
    for copy in copies[PARTS:]:
        copy.wait()
    kept = (zeros, zeros)
    for i in range(2 * LEVELS):
        kept = put(own_statics[i, :, :LANES], own_statics[i, :, LANES:], i, kept)
    flags = own_wet[...].astype(jnp.float32)
    kept = put(flags[:, :LANES], flags[:, LANES:], 2 * LEVELS, kept)
    hand_out(STATIC_LANES, *kept)


def sides(sent_off, sent_on, off_chip, on_chip, lanes):
    odd_block = lax.axis_index("tile") % 2 == 1
    off, on = off_chip[:, lanes], on_chip[:, lanes]
    west, east = jnp.where(odd_block, on, off), jnp.where(odd_block, off, on)
    off, on = sent_off[:, lanes], sent_on[:, lanes]
    own_first, own_last = jnp.where(odd_block, on, off), jnp.where(odd_block, off, on)
    odd = lane_index((ROWS, LANES)) % 2 == 1
    inner = jnp.where(odd, pltpu.roll(own_first, 1, 1), pltpu.roll(own_last, LANES - 1, 1))
    outer = jnp.where(odd, pltpu.roll(west, 1, 1), pltpu.roll(east, LANES - 1, 1))
    return inner, jnp.where(odd, west, east), outer


def repeated(block, start, width):
    lane = lane_index((ROWS, LANES))
    if start:
        block = pltpu.roll(block, LANES - start, 1)
    block = jnp.where(lane < width, block, 0.0)
    while width < LANES:
        block = block + pltpu.roll(block, width, 1)
        width *= 2
    return block


def face(wet, speed, diffuse):
    a = 0.5 * (speed[0] + speed[1])
    k = 0.5 * (diffuse[0] + diffuse[1])
    ocean = wet[0] * wet[1]
    return ocean * (jnp.maximum(a, 0.0) + k), ocean * (jnp.minimum(a, 0.0) - k)


def rows_between(wet, diffuse):
    row = lax.broadcasted_iota(jnp.int32, (ROWS, LANES), 0)
    both = wet * pltpu.roll(wet, ROWS - 1, 0)
    k = 0.5 * (diffuse + pltpu.roll(diffuse, ROWS - 1, 0))
    north = jnp.where(row < ROWS - 1, both * k, 0.0)
    return pltpu.roll(north, 1, 0), north


def five_point(weights, cell, west, east):
    centre, to_west, to_east, above, north = weights
    return (
        centre * cell
        + to_west * west
        + to_east * east
        + above * pltpu.roll(cell, 1, 0)
        + north * pltpu.roll(cell, ROWS - 1, 0)
    )


def border(edges):
    odd = lane_index((ROWS, LANES)) % 2 == 1
    inner, cell, outer = sides(*edges, TRACER_LANES)
    statics = sides(*edges, STATIC_LANES)
    diffuse = [repeated(x, 0, 2 * LEVELS) for x in statics]
    speed = [repeated(x, 2 * LEVELS, 2 * LEVELS) for x in statics]
    wet = [repeated(x, 4 * LEVELS, 2) for x in statics]
    in_west, in_east = face(wet[:2], speed[:2], diffuse[:2])
    out_west, out_east = face(wet[1:], speed[1:], diffuse[1:])
    above, north = rows_between(wet[1], diffuse[1])
    zonal = jnp.where(odd, out_east - in_west, in_east - out_west)
    centre = 1.0 + (zonal - above - north) * wet[1]
    to_inner = jnp.where(odd, -in_east, in_west)
    to_outer = jnp.where(odd, out_west, -out_east)
    stepped = five_point((centre, to_inner, to_outer, above, north), cell, inner, outer)
    return cell, stepped


def neighbours(tiles, halo):
    return bordered(
        [pltpu.roll(tile, 1, 1) for tile in tiles],
        [pltpu.roll(tile, LANES - 1, 1) for tile in tiles],
        halo,
    )


def bordered(west, east, halo):
    lane = lane_index((ROWS, LANES))
    first, last = lane == 0, lane == LANES - 1
    west = [jnp.where(first, halo, west[0]), jnp.where(first, west[0], west[1])]
    return west, [jnp.where(last, east[1], east[0]), jnp.where(last, halo, east[1])]


def turns():
    row = lax.broadcasted_iota(jnp.int32, (2 * LANES, 2 * LANES), 0)
    column = lax.broadcasted_iota(jnp.int32, (2 * LANES, 2 * LANES), 1)
    source = jnp.where(column < LANES, column + LANES - 1, column + 1) % LANES
    return (row % LANES == source).astype(jnp.bfloat16)


def split(block):
    high = block.astype(jnp.bfloat16)
    return high, (block - high.astype(jnp.float32)).astype(jnp.bfloat16)


def aligned(block, index):
    return pltpu.roll(block, LANES - 1 - 2 * index, 1)


def halved(block):
    return [block[:, :LANES], block[:, LANES:]]


def stepper(level, statics, wet, edges):
    cells = sides(*edges, STATIC_LANES)[1]
    ocean = halved(wet[...].astype(jnp.float32))
    diffuse, speed = halved(statics[level]), halved(statics[LEVELS + level])
    (wet_west, wet_east), (diffuse_west, diffuse_east), (speed_west, speed_east) = (
        neighbours(tiles, aligned(cells, index))
        for tiles, index in ((ocean, 2 * LEVELS), (diffuse, level), (speed, LEVELS + level))
    )
    weights = []
    for i in range(2):
        west = face((wet_west[i], ocean[i]), (speed_west[i], speed[i]), (diffuse_west[i], diffuse[i]))
        east = face((ocean[i], wet_east[i]), (speed[i], speed_east[i]), (diffuse[i], diffuse_east[i]))
        above, north = rows_between(ocean[i], diffuse[i])
        centre = 1.0 + (west[1] - east[0] - above - north) * ocean[i]
        weights.append((centre, west[0], -east[1], above, north))

    return weights


def two_steps(weights, turn, planes, borders):
    count = len(planes)
    for halos in borders:
        stacked = jnp.concatenate([tiles[half] for half in range(2) for tiles in planes], 0)
        moved = jnp.dot(
            jnp.concatenate(split(stacked), 1), turn, preferred_element_type=jnp.float32
        )
        stepped = []
        for i in range(count):
            turned = [
                halved(moved[(half * count + i) * ROWS : (half * count + i + 1) * ROWS])
                for half in range(2)
            ]
            west, east = bordered(*zip(*turned), halos[i])
            stepped.append(
                [five_point(weights[h], planes[i][h], west[h], east[h]) for h in range(2)]
            )
        planes = stepped
    return planes


def forecast(state, statics, wet, sent_off, sent_on, off_chip, on_chip, sides_of, chunks):
    edges = (sent_off, sent_on, off_chip, on_chip)
    borders = (sides_of[:ROWS], sides_of[ROWS:])
    turn = turns()

    def level_step(level, carry):
        weights = stepper(level, statics, wet, edges)
        where = [(e, t * LEVELS + level) for e in range(MEMBERS) for t in range(2)]
        planes = [halved(state[e, q]) for e, q in where]
        halos = [[aligned(block, e * PLANES + q) for e, q in where] for block in borders]
        for (e, q), done in zip(where, two_steps(weights, turn, planes, halos)):
            for half in range(2):
                rows = pl.ds(half * HALF_ROWS + e, ROWS, stride=MEMBERS)
                chunks[q, rows, :] = done[half]
        return carry

    lax.fori_loop(0, LEVELS, level_step, 0)


def far():
    place = lax.axis_index("tile") % 4
    return (place == 0) | (place == 3)


def transport(*refs):
    @pl.when(jnp.logical_not(far()))
    def _():
        forecast(*refs)


def observe(
    state, statics, wet, sent_off, sent_on, off_chip, on_chip, cell, value, error, count, out, sides_of
):
    edges = (sent_off, sent_on, off_chip, on_chip)
    borders = border(edges)
    sides_of[:ROWS], sides_of[ROWS:] = borders
    weights = stepper(0, statics, wet, edges)
    planes = [halved(state[e, 0]) for e in range(MEMBERS)]
    halos = [[aligned(block, e * PLANES) for e in range(MEMBERS)] for block in borders]
    surface = [jnp.concatenate(x, 1) for x in two_steps(weights, turns(), planes, halos)]
    in_use = (lane_index((1, SLOTS)) < count[0]).astype(jnp.float32)
    scale = 1.0 / ((ENSEMBLE - 1) * error[...])
    unused = jnp.zeros((5, SLOTS), jnp.float32)
    out[MEMBERS:, :] = jnp.concatenate([in_use, value[...], scale, unused], 0)
    cell = cell[...]
    column = lax.broadcasted_iota(jnp.int32, (COLUMNS, SLOTS), 0)
    pick = (column == (cell & (COLUMNS - 1))).astype(jnp.float32)
    near = jnp.dot(
        jnp.concatenate(surface, 0), pick, precision=HIGHEST, preferred_element_type=jnp.float32
    )
    layer = lax.broadcasted_iota(jnp.int32, (ROWS, SLOTS), 0)
    chosen = layer == (cell >> 8)
    for e in range(MEMBERS):
        kept = jnp.where(chosen, near[e * ROWS : (e + 1) * ROWS], 0.0)
        out[e : e + 1, :] = jnp.sum(kept, 0, keepdims=True)


def attach(chunks, own, off_chip, on_chip, *rest):
    out = rest[-1]

    @pl.when(far())
    def _():
        forecast(*rest)

    for i, block in enumerate((own, off_chip, on_chip)):
        values = block[:MEMBERS]
        for q in range(PLANES):
            out[q, pl.ds(CELL_ROWS + i * MEMBERS, MEMBERS), :] = values


def gram(received, blocks):
    first = lax.broadcasted_iota(jnp.int32, (8, SLOTS), 0) == 0
    unused = jnp.zeros((LANES - ENSEMBLE, SLOTS), jnp.float32)
    left, right = [], []
    for i, (block, locality) in enumerate(zip(blocks, (1.0, 0.5, 0.5))):
        rows = pl.ds(CELL_ROWS + i * MEMBERS, MEMBERS)
        members = received[:, rows, :].reshape(ENSEMBLE, SLOTS)
        in_use, value, scale = (block[MEMBERS + j : MEMBERS + j + 1] for j in range(3))
        mean = jnp.sum(members, 0, keepdims=True) / ENSEMBLE
        anomaly = (members - mean) * in_use
        innovation = (value - mean) * in_use
        left.append(jnp.concatenate([anomaly, jnp.where(first, innovation, 0.0)], 0))
        right.append(jnp.concatenate([anomaly * (scale * locality), unused], 0))
    return lax.dot_general(
        jnp.concatenate(left, 1), jnp.concatenate(right, 1), (((1,), (1,)), ((), ())),
        precision=HIGHEST, preferred_element_type=jnp.float32,
    )


def symmetric_inverse(a, b, c):
    scale = 1.0 / (a * c - b * b)
    return c * scale, -b * scale, a * scale


def pivot_inverse(e):
    a0, a1, a2 = symmetric_inverse(e[0][0], e[0][1], e[1][1])
    b00, b01, b10, b11 = e[0][2], e[0][3], e[1][2], e[1][3]
    f00, f01 = a0 * b00 + a1 * b10, a0 * b01 + a1 * b11
    f10, f11 = a1 * b00 + a2 * b10, a1 * b01 + a2 * b11
    s0, s1, s2 = symmetric_inverse(
        e[2][2] - (b00 * f00 + b10 * f10),
        e[2][3] - (b00 * f01 + b10 * f11),
        e[3][3] - (b01 * f01 + b11 * f11),
    )
    t00, t01 = f00 * s0 + f01 * s1, f00 * s1 + f01 * s2
    t10, t11 = f10 * s0 + f11 * s1, f10 * s1 + f11 * s2
    x01 = a1 + t00 * f10 + t01 * f11
    return [
        [a0 + t00 * f00 + t01 * f01, x01, -t00, -t01],
        [x01, a2 + t10 * f10 + t11 * f11, -t10, -t11],
        [-t00, -t10, s0, s1],
        [-t01, -t11, s1, s2],
    ]


def inverse(tiles):
    row = lax.broadcasted_iota(jnp.int32, (8, LANES), 0)
    lane = lane_index((8, LANES))
    size = 4

    def everywhere(block):
        return jnp.broadcast_to(block, (8, LANES))

    for k in range(0, ENSEMBLE, size):
        home, start = k // 8, k % 8
        columns = [[everywhere(tile[:, k + j : k + j + 1]) for tile in tiles] for j in range(size)]
        rows = [everywhere(tiles[home][start + i : start + i + 1]) for i in range(size)]
        pivots = pivot_inverse(
            [
                [everywhere(columns[j][home][start + i : start + i + 1]) for j in range(size)]
                for i in range(size)
            ]
        )
        scaled = []
        for i in range(size):
            value = (pivots[i][0] * rows[0] + pivots[i][1] * rows[1]) + (
                pivots[i][2] * rows[2] + pivots[i][3] * rows[3]
            )
            for j in range(size):
                value = jnp.where(lane == k + j, pivots[i][j], value)
            scaled.append(value)
        inside = (lane >= k) & (lane < k + size)
        rest = []
        for t, tile in enumerate(tiles):
            value = jnp.where(inside, 0.0, tile)
            for j in range(size):
                value = value - columns[j][t] * scaled[j]
            rest.append(value)
        for i in range(size):
            rest[home] = jnp.where(row == start + i, scaled[i], rest[home])
        tiles = rest
    return jnp.concatenate(tiles, 0)


def analyse(received, own, off_chip, on_chip, out):
    row = lax.broadcasted_iota(jnp.int32, (SYSTEM_ROWS, LANES), 0)
    diagonal = row == lane_index((SYSTEM_ROWS, LANES))
    identity = jnp.where(diagonal & (row < ENSEMBLE), 1.0, 0.0)
    system = identity + gram(received, (own, off_chip, on_chip))
    solved = inverse([system[8 * t : 8 * t + 8] for t in range(SYSTEM_ROWS // 8)])
    weights = 0.5 * (identity + solved)[:ENSEMBLE] - solved[ENSEMBLE : ENSEMBLE + 1]
    high, low = split(weights[:, :ENSEMBLE])
    weights = jnp.concatenate([high, low, high], 1)
    for r in range(ROWS):
        halves = [
            received[:, first : first + MEMBERS, :].reshape(ENSEMBLE, LANES)
            for first in (r * MEMBERS, HALF_ROWS + r * MEMBERS)
        ]
        high, low = split(jnp.concatenate(halves, 1))
        result = jnp.dot(
            weights, jnp.concatenate([high, high, low], 0), preferred_element_type=jnp.float32
        )
        for m in range(ENSEMBLE // MEMBERS):
            rows = result[m * MEMBERS : (m + 1) * MEMBERS]
            out[m, pl.ds(r, MEMBERS, stride=ROWS), :] = rows[:, :LANES]
            out[m, pl.ds(HALF_ROWS + r, MEMBERS, stride=ROWS), :] = rows[:, LANES:]


def unpack(planes, out, left):
    copies = []
    for q in range(PLANES):
        for half in range(2):
            copies.append(
                pltpu.make_async_copy(
                    planes.at[q, half],
                    out.at[:, q, :, half * LANES : (half + 1) * LANES],
                    left.at[q, half],
                )
            )
    for copy in copies:
        copy.start()
    for copy in copies:
        copy.wait()


def vmem():
    return pl.BlockSpec(memory_space=pltpu.VMEM)


def hbm():
    return pl.BlockSpec(memory_space=pltpu.HBM)


def kernel(
    body, operands, *shapes, scalars=(), fetched=(), scratch=(), out_spec=vmem, aliases={}
):
    fetched = [pltpu.with_memory_space_constraint(x, pltpu.HBM) for x in fetched]
    shapes = [s if hasattr(s, "dtype") else jax.ShapeDtypeStruct(s, jnp.float32) for s in shapes]
    return pl.pallas_call(
        body,
        out_shape=shapes,
        in_specs=[vmem()] * len(operands)
        + [pl.BlockSpec(memory_space=pltpu.SMEM)] * len(scalars)
        + [hbm()] * len(fetched),
        out_specs=[out_spec() for _ in shapes],
        scratch_shapes=scratch,
        input_output_aliases=aliases,
        compiler_params=PARAMS,
        name=body.__name__,
    )(*operands, *scalars, *fetched)


def swapped(value, start):
    count = lax.axis_size("tile")
    pairs = [((i + start) % count, (i + 1 + start) % count) for i in range(0, count, 2)]
    return lax.ppermute(value, "tile", pairs + [(b, a) for a, b in pairs])


def both_neighbours(off_chip, on_chip):
    far = swapped(off_chip, 1)
    return far, swapped(on_chip, 0)


def exchanged(value):
    return lax.all_to_all(value, "mem", split_axis=0, concat_axis=0, tiled=True)


def local(
    member_tracer_state, diffusivity, velocity, wet_mask, obs_cell, obs_count, obs_value, obs_error
):
    slot_rows = [x.reshape(1, SLOTS) for x in (obs_cell, obs_value, obs_error)]
    off_chip, on_chip, *blocks, cell, value, error = kernel(
        pack_edges,
        (),
        (ROWS, COLUMNS),
        (ROWS, COLUMNS),
        member_tracer_state.shape,
        (2 * LEVELS, ROWS, COLUMNS),
        jax.ShapeDtypeStruct((ROWS, COLUMNS), jnp.int32),
        jax.ShapeDtypeStruct((1, SLOTS), jnp.int32),
        (1, SLOTS),
        (1, SLOTS),
        fetched=(member_tracer_state, diffusivity, velocity, wet_mask, *slot_rows),
        scratch=[pltpu.SemaphoreType.DMA((PARTS + 6,))],
    )
    edges = (off_chip, on_chip, *both_neighbours(off_chip, on_chip))
    own, sides_of = kernel(
        observe,
        (*blocks, *edges, cell, value, error),
        (2 * MEMBERS, SLOTS),
        (2 * ROWS, LANES),
        scalars=(obs_count,),
    )
    near = (own, *both_neighbours(own, own))
    home = (*blocks, *edges, sides_of)
    (chunks,) = kernel(transport, home, (PLANES, CHUNK_ROWS, LANES))
    (chunks,) = kernel(attach, (chunks, *near, *home), chunks.shape, aliases={0: 0})
    received = exchanged(chunks)
    (updated,) = kernel(analyse, (received, *near), (PLANES, CELL_ROWS, LANES))
    back = exchanged(updated)
    (analysis,) = kernel(
        unpack,
        (back.reshape(PLANES, 2, MEMBERS, ROWS, LANES),),
        member_tracer_state.shape,
        scratch=[pltpu.SemaphoreType.DMA((PLANES, 2))],
        out_spec=hbm,
    )
    return analysis


def solution(mesh):
    in_specs = (
        P("mem", None, None, "tile"),
        P(None, None, "tile"),
        P(None, None, "tile"),
        P(None, "tile"),
        P("tile"),
        P("tile"),
        P("tile"),
        P("tile"),
    )
    out_specs = P("mem", None, None, "tile")
    return jax.shard_map(local, mesh=mesh, in_specs=in_specs, out_specs=out_specs, check_vma=False)
```

```python
import jax
import jax.numpy as jnp
from jax import lax
from jax.experimental import pallas as pl
from jax.experimental.pallas import tpu as pltpu
from jax.sharding import PartitionSpec as P

LEVELS = 4
PLANES = 8
MEMBERS = 8
PARTS = 4
ENSEMBLE = 64
ROWS = 16
COLUMNS = 256
SLOTS = 128
LANES = 128
HALF_ROWS = ROWS * MEMBERS
CELL_ROWS = 2 * HALF_ROWS
CHUNK_ROWS = CELL_ROWS + 3 * MEMBERS
SYSTEM_ROWS = ENSEMBLE + 8
TRACER_LANES, STATIC_LANES = slice(0, LANES), slice(LANES, 2 * LANES)
HIGHEST = lax.Precision.HIGHEST
PARAMS = pltpu.CompilerParams(vmem_limit_bytes=32 * 1024 * 1024)


def lane_index(shape):
    return lax.broadcasted_iota(jnp.int32, shape, 1)


def pack_edges(
    state, diffusivity, velocity, wet, cell, value, error, off_chip, on_chip, own_state, own_statics,
    own_wet, own_cell, own_value, own_error, arrived
):
    odd = lax.axis_index("tile") % 2 == 1

    def hand_out(lanes, first, last):
        on_chip[:, lanes] = jnp.where(odd, first, last)
        off_chip[:, lanes] = jnp.where(odd, last, first)

    copies = []
    for part in range(PARTS):
        rows = slice(part * MEMBERS // PARTS, (part + 1) * MEMBERS // PARTS)
        copies.append((state.at[rows], own_state.at[rows]))
    copies += [
        (diffusivity, own_statics.at[:LEVELS]),
        (velocity, own_statics.at[LEVELS:]),
        (wet, own_wet),
        (cell, own_cell),
        (value, own_value),
        (error, own_error),
    ]
    copies = [
        pltpu.make_async_copy(source, target, arrived.at[i])
        for i, (source, target) in enumerate(copies)
    ]
    for copy in copies:
        copy.start()
    pair = lane_index((ROWS, LANES)) >> 1

    def put(low, high, index, kept):
        first_kept, last_kept = kept
        first_kept = jnp.where(pair == index, pltpu.roll(low, 2 * index, 1), first_kept)
        last_kept = jnp.where(
            pair == index, pltpu.roll(high, (2 * index + 2) % LANES, 1), last_kept
        )
        return first_kept, last_kept

    def member(e, kept):
        for q in range(PLANES):
            low, high = own_state[e, q, :, :LANES], own_state[e, q, :, LANES:]
            kept = put(low, high, e * PLANES + q, kept)
        return kept

    zeros = jnp.zeros((ROWS, LANES), jnp.float32)
    kept = (zeros, zeros)
    for part in range(PARTS):
        copies[part].wait()
        rows = range(part * MEMBERS // PARTS, (part + 1) * MEMBERS // PARTS)
        for e in rows:
            kept = member(e, kept)
    hand_out(TRACER_LANES, *kept)
    for copy in copies[PARTS:]:
        copy.wait()
    kept = (zeros, zeros)
    for i in range(2 * LEVELS):
        kept = put(own_statics[i, :, :LANES], own_statics[i, :, LANES:], i, kept)
    flags = own_wet[...].astype(jnp.float32)
    kept = put(flags[:, :LANES], flags[:, LANES:], 2 * LEVELS, kept)
    hand_out(STATIC_LANES, *kept)


def sides(sent_off, sent_on, off_chip, on_chip, lanes):
    odd_block = lax.axis_index("tile") % 2 == 1
    off, on = off_chip[:, lanes], on_chip[:, lanes]
    west, east = jnp.where(odd_block, on, off), jnp.where(odd_block, off, on)
    off, on = sent_off[:, lanes], sent_on[:, lanes]
    own_first, own_last = jnp.where(odd_block, on, off), jnp.where(odd_block, off, on)
    odd = lane_index((ROWS, LANES)) % 2 == 1
    inner = jnp.where(odd, pltpu.roll(own_first, 1, 1), pltpu.roll(own_last, LANES - 1, 1))
    outer = jnp.where(odd, pltpu.roll(west, 1, 1), pltpu.roll(east, LANES - 1, 1))
    return inner, jnp.where(odd, west, east), outer


def repeated(block, start, width):
    lane = lane_index((ROWS, LANES))
    if start:
        block = pltpu.roll(block, LANES - start, 1)
    block = jnp.where(lane < width, block, 0.0)
    while width < LANES:
        block = block + pltpu.roll(block, width, 1)
        width *= 2
    return block


def face(wet, speed, diffuse):
    a = 0.5 * (speed[0] + speed[1])
    k = 0.5 * (diffuse[0] + diffuse[1])
    ocean = wet[0] * wet[1]
    return ocean * (jnp.maximum(a, 0.0) + k), ocean * (jnp.minimum(a, 0.0) - k)


def rows_between(wet, diffuse):
    row = lax.broadcasted_iota(jnp.int32, (ROWS, LANES), 0)
    both = wet * pltpu.roll(wet, ROWS - 1, 0)
    k = 0.5 * (diffuse + pltpu.roll(diffuse, ROWS - 1, 0))
    north = jnp.where(row < ROWS - 1, both * k, 0.0)
    return pltpu.roll(north, 1, 0), north


def five_point(weights, cell, west, east):
    centre, to_west, to_east, above, north = weights
    return (
        centre * cell
        + to_west * west
        + to_east * east
        + above * pltpu.roll(cell, 1, 0)
        + north * pltpu.roll(cell, ROWS - 1, 0)
    )


def border(edges):
    odd = lane_index((ROWS, LANES)) % 2 == 1
    inner, cell, outer = sides(*edges, TRACER_LANES)
    statics = sides(*edges, STATIC_LANES)
    diffuse = [repeated(x, 0, 2 * LEVELS) for x in statics]
    speed = [repeated(x, 2 * LEVELS, 2 * LEVELS) for x in statics]
    wet = [repeated(x, 4 * LEVELS, 2) for x in statics]
    in_west, in_east = face(wet[:2], speed[:2], diffuse[:2])
    out_west, out_east = face(wet[1:], speed[1:], diffuse[1:])
    above, north = rows_between(wet[1], diffuse[1])
    zonal = jnp.where(odd, out_east - in_west, in_east - out_west)
    centre = 1.0 + (zonal - above - north) * wet[1]
    to_inner = jnp.where(odd, -in_east, in_west)
    to_outer = jnp.where(odd, out_west, -out_east)
    stepped = five_point((centre, to_inner, to_outer, above, north), cell, inner, outer)
    return cell, stepped


def neighbours(tiles, halo):
    return bordered(
        [pltpu.roll(tile, 1, 1) for tile in tiles],
        [pltpu.roll(tile, LANES - 1, 1) for tile in tiles],
        halo,
    )


def bordered(west, east, halo):
    lane = lane_index((ROWS, LANES))
    first, last = lane == 0, lane == LANES - 1
    west = [jnp.where(first, halo, west[0]), jnp.where(first, west[0], west[1])]
    return west, [jnp.where(last, east[1], east[0]), jnp.where(last, halo, east[1])]


def turns():
    row = lax.broadcasted_iota(jnp.int32, (3 * LANES, 2 * LANES), 0)
    column = lax.broadcasted_iota(jnp.int32, (3 * LANES, 2 * LANES), 1)
    source = jnp.where(column < LANES, column + LANES - 1, column + 1) % LANES
    return (row % LANES == source).astype(jnp.bfloat16)


def split(block, count):
    parts = []
    for i in range(count):
        parts.append(block.astype(jnp.bfloat16))
        block = block - parts[-1].astype(jnp.float32)
    return parts


def aligned(block, index):
    return pltpu.roll(block, LANES - 1 - 2 * index, 1)


def halved(block):
    return [block[:, :LANES], block[:, LANES:]]


def stepper(level, statics, wet, edges):
    cells = sides(*edges, STATIC_LANES)[1]
    ocean = halved(wet[...].astype(jnp.float32))
    diffuse, speed = halved(statics[level]), halved(statics[LEVELS + level])
    (wet_west, wet_east), (diffuse_west, diffuse_east), (speed_west, speed_east) = (
        neighbours(tiles, aligned(cells, index))
        for tiles, index in ((ocean, 2 * LEVELS), (diffuse, level), (speed, LEVELS + level))
    )
    weights = []
    for i in range(2):
        west = face((wet_west[i], ocean[i]), (speed_west[i], speed[i]), (diffuse_west[i], diffuse[i]))
        east = face((ocean[i], wet_east[i]), (speed[i], speed_east[i]), (diffuse[i], diffuse_east[i]))
        above, north = rows_between(ocean[i], diffuse[i])
        centre = 1.0 + (west[1] - east[0] - above - north) * ocean[i]
        weights.append((centre, west[0], -east[1], above, north))

    return weights


def two_steps(weights, turn, planes, borders):
    count = len(planes)
    for halos in borders:
        stacked = jnp.concatenate([tiles[half] for half in range(2) for tiles in planes], 0)
        moved = jnp.dot(
            jnp.concatenate(split(stacked, 3), 1), turn, preferred_element_type=jnp.float32
        )
        stepped = []
        for i in range(count):
            turned = [
                halved(moved[(half * count + i) * ROWS : (half * count + i + 1) * ROWS])
                for half in range(2)
            ]
            west, east = bordered(*zip(*turned), halos[i])
            stepped.append(
                [five_point(weights[h], planes[i][h], west[h], east[h]) for h in range(2)]
            )
        planes = stepped
    return planes


def forecast(state, statics, wet, sent_off, sent_on, off_chip, on_chip, sides_of, chunks):
    edges = (sent_off, sent_on, off_chip, on_chip)
    borders = (sides_of[:ROWS], sides_of[ROWS:])
    turn = turns()

    def level_step(level, carry):
        weights = stepper(level, statics, wet, edges)
        where = [(e, t * LEVELS + level) for e in range(MEMBERS) for t in range(2)]
        planes = [halved(state[e, q]) for e, q in where]
        halos = [[aligned(block, e * PLANES + q) for e, q in where] for block in borders]
        for (e, q), done in zip(where, two_steps(weights, turn, planes, halos)):
            for half in range(2):
                rows = pl.ds(half * HALF_ROWS + e, ROWS, stride=MEMBERS)
                chunks[q, rows, :] = done[half]
        return carry

    lax.fori_loop(0, LEVELS, level_step, 0)


def far():
    place = lax.axis_index("tile") % 4
    return (place == 0) | (place == 3)


def transport(*refs):
    @pl.when(jnp.logical_not(far()))
    def _():
        forecast(*refs)


def observe(
    state, statics, wet, sent_off, sent_on, off_chip, on_chip, cell, value, error, count, out, sides_of
):
    edges = (sent_off, sent_on, off_chip, on_chip)
    borders = border(edges)
    sides_of[:ROWS], sides_of[ROWS:] = borders
    weights = stepper(0, statics, wet, edges)
    planes = [halved(state[e, 0]) for e in range(MEMBERS)]
    halos = [[aligned(block, e * PLANES) for e in range(MEMBERS)] for block in borders]
    surface = [jnp.concatenate(x, 1) for x in two_steps(weights, turns(), planes, halos)]
    in_use = (lane_index((1, SLOTS)) < count[0]).astype(jnp.float32)
    scale = 1.0 / ((ENSEMBLE - 1) * error[...])
    unused = jnp.zeros((5, SLOTS), jnp.float32)
    out[MEMBERS:, :] = jnp.concatenate([in_use, value[...], scale, unused], 0)
    cell = cell[...]
    column = lax.broadcasted_iota(jnp.int32, (COLUMNS, SLOTS), 0)
    pick = (column == (cell & (COLUMNS - 1))).astype(jnp.float32)
    near = jnp.dot(
        jnp.concatenate(surface, 0), pick, precision=HIGHEST, preferred_element_type=jnp.float32
    )
    layer = lax.broadcasted_iota(jnp.int32, (ROWS, SLOTS), 0)
    chosen = layer == (cell >> 8)
    for e in range(MEMBERS):
        kept = jnp.where(chosen, near[e * ROWS : (e + 1) * ROWS], 0.0)
        out[e : e + 1, :] = jnp.sum(kept, 0, keepdims=True)


def attach(chunks, own, off_chip, on_chip, *rest):
    out = rest[-1]

    @pl.when(far())
    def _():
        forecast(*rest)

    for i, block in enumerate((own, off_chip, on_chip)):
        values = block[:MEMBERS]
        for q in range(PLANES):
            out[q, pl.ds(CELL_ROWS + i * MEMBERS, MEMBERS), :] = values


def gram(received, blocks):
    first = lax.broadcasted_iota(jnp.int32, (8, SLOTS), 0) == 0
    unused = jnp.zeros((LANES - ENSEMBLE, SLOTS), jnp.float32)
    left, right = [], []
    for i, (block, locality) in enumerate(zip(blocks, (1.0, 0.5, 0.5))):
        rows = pl.ds(CELL_ROWS + i * MEMBERS, MEMBERS)
        members = received[:, rows, :].reshape(ENSEMBLE, SLOTS)
        in_use, value, scale = (block[MEMBERS + j : MEMBERS + j + 1] for j in range(3))
        mean = jnp.sum(members, 0, keepdims=True) / ENSEMBLE
        anomaly = (members - mean) * in_use
        innovation = (value - mean) * in_use
        left.append(jnp.concatenate([anomaly, jnp.where(first, innovation, 0.0)], 0))
        right.append(jnp.concatenate([anomaly * (scale * locality), unused], 0))
    return lax.dot_general(
        jnp.concatenate(left, 1), jnp.concatenate(right, 1), (((1,), (1,)), ((), ())),
        precision=HIGHEST, preferred_element_type=jnp.float32,
    )


def symmetric_inverse(a, b, c):
    scale = 1.0 / (a * c - b * b)
    return c * scale, -b * scale, a * scale


def pivot_inverse(e):
    a0, a1, a2 = symmetric_inverse(e[0][0], e[0][1], e[1][1])
    b00, b01, b10, b11 = e[0][2], e[0][3], e[1][2], e[1][3]
    f00, f01 = a0 * b00 + a1 * b10, a0 * b01 + a1 * b11
    f10, f11 = a1 * b00 + a2 * b10, a1 * b01 + a2 * b11
    s0, s1, s2 = symmetric_inverse(
        e[2][2] - (b00 * f00 + b10 * f10),
        e[2][3] - (b00 * f01 + b10 * f11),
        e[3][3] - (b01 * f01 + b11 * f11),
    )
    t00, t01 = f00 * s0 + f01 * s1, f00 * s1 + f01 * s2
    t10, t11 = f10 * s0 + f11 * s1, f10 * s1 + f11 * s2
    x01 = a1 + t00 * f10 + t01 * f11
    return [
        [a0 + t00 * f00 + t01 * f01, x01, -t00, -t01],
        [x01, a2 + t10 * f10 + t11 * f11, -t10, -t11],
        [-t00, -t10, s0, s1],
        [-t01, -t11, s1, s2],
    ]


def inverse(tiles):
    row = lax.broadcasted_iota(jnp.int32, (8, LANES), 0)
    lane = lane_index((8, LANES))
    size = 4

    def everywhere(block):
        return jnp.broadcast_to(block, (8, LANES))

    for k in range(0, ENSEMBLE, size):
        home, start = k // 8, k % 8
        columns = [[everywhere(tile[:, k + j : k + j + 1]) for tile in tiles] for j in range(size)]
        rows = [everywhere(tiles[home][start + i : start + i + 1]) for i in range(size)]
        pivots = pivot_inverse(
            [
                [everywhere(columns[j][home][start + i : start + i + 1]) for j in range(size)]
                for i in range(size)
            ]
        )
        scaled = []
        for i in range(size):
            value = (pivots[i][0] * rows[0] + pivots[i][1] * rows[1]) + (
                pivots[i][2] * rows[2] + pivots[i][3] * rows[3]
            )
            for j in range(size):
                value = jnp.where(lane == k + j, pivots[i][j], value)
            scaled.append(value)
        inside = (lane >= k) & (lane < k + size)
        rest = []
        for t, tile in enumerate(tiles):
            value = jnp.where(inside, 0.0, tile)
            for j in range(size):
                value = value - columns[j][t] * scaled[j]
            rest.append(value)
        for i in range(size):
            rest[home] = jnp.where(row == start + i, scaled[i], rest[home])
        tiles = rest
    return jnp.concatenate(tiles, 0)


def analyse(received, own, off_chip, on_chip, out):
    row = lax.broadcasted_iota(jnp.int32, (SYSTEM_ROWS, LANES), 0)
    diagonal = row == lane_index((SYSTEM_ROWS, LANES))
    identity = jnp.where(diagonal & (row < ENSEMBLE), 1.0, 0.0)
    system = identity + gram(received, (own, off_chip, on_chip))
    solved = inverse([system[8 * t : 8 * t + 8] for t in range(SYSTEM_ROWS // 8)])
    weights = 0.5 * (solved - identity)[:ENSEMBLE] - solved[ENSEMBLE : ENSEMBLE + 1]
    high, low = split(weights[:, :ENSEMBLE], 2)
    weights = jnp.concatenate([high, low, high], 1)
    for r in range(ROWS):
        members = jnp.concatenate(
            [
                received[:, first : first + MEMBERS, :].reshape(ENSEMBLE, LANES)
                for first in (r * MEMBERS, HALF_ROWS + r * MEMBERS)
            ],
            1,
        )
        mean = jnp.sum(members, 0, keepdims=True) / ENSEMBLE
        high, low = split(members - mean, 2)
        result = members + jnp.dot(
            weights, jnp.concatenate([high, high, low], 0), preferred_element_type=jnp.float32
        )
        for m in range(ENSEMBLE // MEMBERS):
            rows = result[m * MEMBERS : (m + 1) * MEMBERS]
            out[m, pl.ds(r, MEMBERS, stride=ROWS), :] = rows[:, :LANES]
            out[m, pl.ds(HALF_ROWS + r, MEMBERS, stride=ROWS), :] = rows[:, LANES:]


def unpack(planes, out, left):
    copies = []
    for q in range(PLANES):
        for half in range(2):
            copies.append(
                pltpu.make_async_copy(
                    planes.at[q, half],
                    out.at[:, q, :, half * LANES : (half + 1) * LANES],
                    left.at[q, half],
                )
            )
    for copy in copies:
        copy.start()
    for copy in copies:
        copy.wait()


def vmem():
    return pl.BlockSpec(memory_space=pltpu.VMEM)


def hbm():
    return pl.BlockSpec(memory_space=pltpu.HBM)


def kernel(
    body, operands, *shapes, scalars=(), fetched=(), scratch=(), out_spec=vmem, aliases={}
):
    fetched = [pltpu.with_memory_space_constraint(x, pltpu.HBM) for x in fetched]
    shapes = [s if hasattr(s, "dtype") else jax.ShapeDtypeStruct(s, jnp.float32) for s in shapes]
    return pl.pallas_call(
        body,
        out_shape=shapes,
        in_specs=[vmem()] * len(operands)
        + [pl.BlockSpec(memory_space=pltpu.SMEM)] * len(scalars)
        + [hbm()] * len(fetched),
        out_specs=[out_spec() for _ in shapes],
        scratch_shapes=scratch,
        input_output_aliases=aliases,
        compiler_params=PARAMS,
        name=body.__name__,
    )(*operands, *scalars, *fetched)


def swapped(value, start):
    count = lax.axis_size("tile")
    pairs = [((i + start) % count, (i + 1 + start) % count) for i in range(0, count, 2)]
    return lax.ppermute(value, "tile", pairs + [(b, a) for a, b in pairs])


def both_neighbours(off_chip, on_chip):
    far = swapped(off_chip, 1)
    return far, swapped(on_chip, 0)


def exchanged(value):
    return lax.all_to_all(value, "mem", split_axis=0, concat_axis=0, tiled=True)


def local(
    member_tracer_state, diffusivity, velocity, wet_mask, obs_cell, obs_count, obs_value, obs_error
):
    slot_rows = [x.reshape(1, SLOTS) for x in (obs_cell, obs_value, obs_error)]
    off_chip, on_chip, *blocks, cell, value, error = kernel(
        pack_edges,
        (),
        (ROWS, COLUMNS),
        (ROWS, COLUMNS),
        member_tracer_state.shape,
        (2 * LEVELS, ROWS, COLUMNS),
        jax.ShapeDtypeStruct((ROWS, COLUMNS), jnp.int32),
        jax.ShapeDtypeStruct((1, SLOTS), jnp.int32),
        (1, SLOTS),
        (1, SLOTS),
        fetched=(member_tracer_state, diffusivity, velocity, wet_mask, *slot_rows),
        scratch=[pltpu.SemaphoreType.DMA((PARTS + 6,))],
    )
    edges = (off_chip, on_chip, *both_neighbours(off_chip, on_chip))
    own, sides_of = kernel(
        observe,
        (*blocks, *edges, cell, value, error),
        (2 * MEMBERS, SLOTS),
        (2 * ROWS, LANES),
        scalars=(obs_count,),
    )
    near = (own, *both_neighbours(own, own))
    home = (*blocks, *edges, sides_of)
    (chunks,) = kernel(transport, home, (PLANES, CHUNK_ROWS, LANES))
    (chunks,) = kernel(attach, (chunks, *near, *home), chunks.shape, aliases={0: 0})
    received = exchanged(chunks)
    (updated,) = kernel(analyse, (received, *near), (PLANES, CELL_ROWS, LANES))
    back = exchanged(updated)
    (analysis,) = kernel(
        unpack,
        (back.reshape(PLANES, 2, MEMBERS, ROWS, LANES),),
        member_tracer_state.shape,
        scratch=[pltpu.SemaphoreType.DMA((PLANES, 2))],
        out_spec=hbm,
    )
    return analysis


def solution(mesh):
    in_specs = (
        P("mem", None, None, "tile"),
        P(None, None, "tile"),
        P(None, None, "tile"),
        P(None, "tile"),
        P("tile"),
        P("tile"),
        P("tile"),
        P("tile"),
    )
    out_specs = P("mem", None, None, "tile")
    return jax.shard_map(local, mesh=mesh, in_specs=in_specs, out_specs=out_specs, check_vma=False)
```

```python
import jax
import jax.numpy as jnp
from jax import lax
from jax.experimental import pallas as pl
from jax.experimental.pallas import tpu as pltpu
from jax.sharding import PartitionSpec as P

LEVELS = 4
PLANES = 8
MEMBERS = 8
PARTS = 4
ENSEMBLE = 64
ROWS = 16
COLUMNS = 256
SLOTS = 128
LANES = 128
HALF_ROWS = ROWS * MEMBERS
CELL_ROWS = 2 * HALF_ROWS
CHUNK_ROWS = CELL_ROWS + 3 * MEMBERS
SYSTEM_ROWS = ENSEMBLE + 8
TRACER_LANES, STATIC_LANES = slice(0, LANES), slice(LANES, 2 * LANES)
HIGHEST = lax.Precision.HIGHEST
PARAMS = pltpu.CompilerParams(vmem_limit_bytes=32 * 1024 * 1024)


def lane_index(shape):
    return lax.broadcasted_iota(jnp.int32, shape, 1)


def pack_edges(
    state, diffusivity, velocity, wet, cell, value, error, off_chip, on_chip, own_state, own_statics,
    own_wet, own_cell, own_value, own_error, arrived
):
    odd = lax.axis_index("tile") % 2 == 1

    def hand_out(lanes, first, last):
        on_chip[:, lanes] = jnp.where(odd, first, last)
        off_chip[:, lanes] = jnp.where(odd, last, first)

    copies = []
    for part in range(PARTS):
        rows = slice(part * MEMBERS // PARTS, (part + 1) * MEMBERS // PARTS)
        copies.append((state.at[rows], own_state.at[rows]))
    copies += [
        (diffusivity, own_statics.at[:LEVELS]),
        (velocity, own_statics.at[LEVELS:]),
        (wet, own_wet),
        (cell, own_cell),
        (value, own_value),
        (error, own_error),
    ]
    copies = [
        pltpu.make_async_copy(source, target, arrived.at[i])
        for i, (source, target) in enumerate(copies)
    ]
    for copy in copies:
        copy.start()
    pair = lane_index((ROWS, LANES)) >> 1

    def put(low, high, index, kept):
        first_kept, last_kept = kept
        first_kept = jnp.where(pair == index, pltpu.roll(low, 2 * index, 1), first_kept)
        last_kept = jnp.where(
            pair == index, pltpu.roll(high, (2 * index + 2) % LANES, 1), last_kept
        )
        return first_kept, last_kept

    def member(e, kept):
        for q in range(PLANES):
            low, high = own_state[e, q, :, :LANES], own_state[e, q, :, LANES:]
            kept = put(low, high, e * PLANES + q, kept)
        return kept

    zeros = jnp.zeros((ROWS, LANES), jnp.float32)
    kept = (zeros, zeros)
    for part in range(PARTS):
        copies[part].wait()
        rows = range(part * MEMBERS // PARTS, (part + 1) * MEMBERS // PARTS)
        for e in rows:
            kept = member(e, kept)
    hand_out(TRACER_LANES, *kept)
    for copy in copies[PARTS:]:
        copy.wait()
    kept = (zeros, zeros)
    for i in range(2 * LEVELS):
        kept = put(own_statics[i, :, :LANES], own_statics[i, :, LANES:], i, kept)
    flags = own_wet[...].astype(jnp.float32)
    kept = put(flags[:, :LANES], flags[:, LANES:], 2 * LEVELS, kept)
    hand_out(STATIC_LANES, *kept)


def sides(sent_off, sent_on, off_chip, on_chip, lanes):
    odd_block = lax.axis_index("tile") % 2 == 1
    off, on = off_chip[:, lanes], on_chip[:, lanes]
    west, east = jnp.where(odd_block, on, off), jnp.where(odd_block, off, on)
    off, on = sent_off[:, lanes], sent_on[:, lanes]
    own_first, own_last = jnp.where(odd_block, on, off), jnp.where(odd_block, off, on)
    odd = lane_index((ROWS, LANES)) % 2 == 1
    inner = jnp.where(odd, pltpu.roll(own_first, 1, 1), pltpu.roll(own_last, LANES - 1, 1))
    outer = jnp.where(odd, pltpu.roll(west, 1, 1), pltpu.roll(east, LANES - 1, 1))
    return inner, jnp.where(odd, west, east), outer


def repeated(block, start, width):
    lane = lane_index((ROWS, LANES))
    if start:
        block = pltpu.roll(block, LANES - start, 1)
    block = jnp.where(lane < width, block, 0.0)
    while width < LANES:
        block = block + pltpu.roll(block, width, 1)
        width *= 2
    return block


def face(wet, speed, diffuse):
    a = 0.5 * (speed[0] + speed[1])
    k = 0.5 * (diffuse[0] + diffuse[1])
    ocean = wet[0] * wet[1]
    return ocean * (jnp.maximum(a, 0.0) + k), ocean * (jnp.minimum(a, 0.0) - k)


def rows_between(wet, diffuse):
    row = lax.broadcasted_iota(jnp.int32, (ROWS, LANES), 0)
    both = wet * pltpu.roll(wet, ROWS - 1, 0)
    k = 0.5 * (diffuse + pltpu.roll(diffuse, ROWS - 1, 0))
    north = jnp.where(row < ROWS - 1, both * k, 0.0)
    return pltpu.roll(north, 1, 0), north


def five_point(weights, cell, west, east):
    centre, to_west, to_east, above, north = weights
    return (
        centre * cell
        + to_west * west
        + to_east * east
        + above * pltpu.roll(cell, 1, 0)
        + north * pltpu.roll(cell, ROWS - 1, 0)
    )


def border(edges):
    odd = lane_index((ROWS, LANES)) % 2 == 1
    inner, cell, outer = sides(*edges, TRACER_LANES)
    statics = sides(*edges, STATIC_LANES)
    diffuse = [repeated(x, 0, 2 * LEVELS) for x in statics]
    speed = [repeated(x, 2 * LEVELS, 2 * LEVELS) for x in statics]
    wet = [repeated(x, 4 * LEVELS, 2) for x in statics]
    in_west, in_east = face(wet[:2], speed[:2], diffuse[:2])
    out_west, out_east = face(wet[1:], speed[1:], diffuse[1:])
    above, north = rows_between(wet[1], diffuse[1])
    zonal = jnp.where(odd, out_east - in_west, in_east - out_west)
    centre = 1.0 + (zonal - above - north) * wet[1]
    to_inner = jnp.where(odd, -in_east, in_west)
    to_outer = jnp.where(odd, out_west, -out_east)
    stepped = five_point((centre, to_inner, to_outer, above, north), cell, inner, outer)
    return cell, stepped


def neighbours(tiles, halo):
    return bordered(
        [pltpu.roll(tile, 1, 1) for tile in tiles],
        [pltpu.roll(tile, LANES - 1, 1) for tile in tiles],
        halo,
    )


def bordered(west, east, halo):
    lane = lane_index((ROWS, LANES))
    first, last = lane == 0, lane == LANES - 1
    west = [jnp.where(first, halo, west[0]), jnp.where(first, west[0], west[1])]
    return west, [jnp.where(last, east[1], east[0]), jnp.where(last, halo, east[1])]


def turns():
    row = lax.broadcasted_iota(jnp.int32, (3 * LANES, 2 * LANES), 0)
    column = lax.broadcasted_iota(jnp.int32, (3 * LANES, 2 * LANES), 1)
    source = jnp.where(column < LANES, column + LANES - 1, column + 1) % LANES
    return (row % LANES == source).astype(jnp.bfloat16)


def split(block, count):
    parts = []
    for i in range(count):
        parts.append(block.astype(jnp.bfloat16))
        block = block - parts[-1].astype(jnp.float32)
    return parts


def aligned(block, index):
    return pltpu.roll(block, LANES - 1 - 2 * index, 1)


def halved(block):
    return [block[:, :LANES], block[:, LANES:]]


def stepper(level, statics, wet, edges):
    cells = sides(*edges, STATIC_LANES)[1]
    ocean = halved(wet[...].astype(jnp.float32))
    diffuse, speed = halved(statics[level]), halved(statics[LEVELS + level])
    (wet_west, wet_east), (diffuse_west, diffuse_east), (speed_west, speed_east) = (
        neighbours(tiles, aligned(cells, index))
        for tiles, index in ((ocean, 2 * LEVELS), (diffuse, level), (speed, LEVELS + level))
    )
    weights = []
    for i in range(2):
        west = face((wet_west[i], ocean[i]), (speed_west[i], speed[i]), (diffuse_west[i], diffuse[i]))
        east = face((ocean[i], wet_east[i]), (speed[i], speed_east[i]), (diffuse[i], diffuse_east[i]))
        above, north = rows_between(ocean[i], diffuse[i])
        centre = 1.0 + (west[1] - east[0] - above - north) * ocean[i]
        weights.append((centre, west[0], -east[1], above, north))

    return weights


def two_steps(weights, turn, planes, borders):
    count = len(planes) // 2
    for halos in borders:
        stacked = jnp.concatenate([tiles[half] for half in range(2) for tiles in planes[:count]], 0)
        moved = jnp.dot(
            jnp.concatenate(split(stacked, 3), 1), turn, preferred_element_type=jnp.float32
        )
        stepped = []
        for i, tiles in enumerate(planes):
            if i < count:
                turned = [
                    halved(moved[(half * count + i) * ROWS : (half * count + i + 1) * ROWS])
                    for half in range(2)
                ]
                west, east = bordered(*zip(*turned), halos[i])
            else:
                west, east = neighbours(tiles, halos[i])
            stepped.append([five_point(weights[h], tiles[h], west[h], east[h]) for h in range(2)])
        planes = stepped
    return planes


def forecast(state, statics, wet, sent_off, sent_on, off_chip, on_chip, sides_of, chunks):
    edges = (sent_off, sent_on, off_chip, on_chip)
    borders = (sides_of[:ROWS], sides_of[ROWS:])
    turn = turns()

    def level_step(level, carry):
        weights = stepper(level, statics, wet, edges)
        where = [(e, t * LEVELS + level) for e in range(MEMBERS) for t in range(2)]
        planes = [halved(state[e, q]) for e, q in where]
        halos = [[aligned(block, e * PLANES + q) for e, q in where] for block in borders]
        for (e, q), done in zip(where, two_steps(weights, turn, planes, halos)):
            for half in range(2):
                rows = pl.ds(half * HALF_ROWS + e, ROWS, stride=MEMBERS)
                chunks[q, rows, :] = done[half]
        return carry

    lax.fori_loop(0, LEVELS, level_step, 0)


def far():
    place = lax.axis_index("tile") % 4
    return (place == 0) | (place == 3)


def transport(*refs):
    @pl.when(jnp.logical_not(far()))
    def _():
        forecast(*refs)


def observe(
    state, statics, wet, sent_off, sent_on, off_chip, on_chip, cell, value, error, count, out, sides_of
):
    edges = (sent_off, sent_on, off_chip, on_chip)
    borders = border(edges)
    sides_of[:ROWS], sides_of[ROWS:] = borders
    weights = stepper(0, statics, wet, edges)
    planes = [halved(state[e, 0]) for e in range(MEMBERS)]
    halos = [[aligned(block, e * PLANES) for e in range(MEMBERS)] for block in borders]
    surface = [jnp.concatenate(x, 1) for x in two_steps(weights, turns(), planes, halos)]
    in_use = (lane_index((1, SLOTS)) < count[0]).astype(jnp.float32)
    scale = 1.0 / ((ENSEMBLE - 1) * error[...])
    unused = jnp.zeros((5, SLOTS), jnp.float32)
    out[MEMBERS:, :] = jnp.concatenate([in_use, value[...], scale, unused], 0)
    cell = cell[...]
    column = lax.broadcasted_iota(jnp.int32, (COLUMNS, SLOTS), 0)
    pick = (column == (cell & (COLUMNS - 1))).astype(jnp.float32)
    near = jnp.dot(
        jnp.concatenate(surface, 0), pick, precision=HIGHEST, preferred_element_type=jnp.float32
    )
    layer = lax.broadcasted_iota(jnp.int32, (ROWS, SLOTS), 0)
    chosen = layer == (cell >> 8)
    for e in range(MEMBERS):
        kept = jnp.where(chosen, near[e * ROWS : (e + 1) * ROWS], 0.0)
        out[e : e + 1, :] = jnp.sum(kept, 0, keepdims=True)


def attach(chunks, own, off_chip, on_chip, *rest):
    out = rest[-1]

    @pl.when(far())
    def _():
        forecast(*rest)

    for i, block in enumerate((own, off_chip, on_chip)):
        values = block[:MEMBERS]
        for q in range(PLANES):
            out[q, pl.ds(CELL_ROWS + i * MEMBERS, MEMBERS), :] = values


def gram(received, blocks):
    first = lax.broadcasted_iota(jnp.int32, (8, SLOTS), 0) == 0
    unused = jnp.zeros((LANES - ENSEMBLE, SLOTS), jnp.float32)
    left, right = [], []
    for i, (block, locality) in enumerate(zip(blocks, (1.0, 0.5, 0.5))):
        rows = pl.ds(CELL_ROWS + i * MEMBERS, MEMBERS)
        members = received[:, rows, :].reshape(ENSEMBLE, SLOTS)
        in_use, value, scale = (block[MEMBERS + j : MEMBERS + j + 1] for j in range(3))
        mean = jnp.sum(members, 0, keepdims=True) / ENSEMBLE
        anomaly = (members - mean) * in_use
        innovation = (value - mean) * in_use
        left.append(jnp.concatenate([anomaly, jnp.where(first, innovation, 0.0)], 0))
        right.append(jnp.concatenate([anomaly * (scale * locality), unused], 0))
    return lax.dot_general(
        jnp.concatenate(left, 1), jnp.concatenate(right, 1), (((1,), (1,)), ((), ())),
        precision=HIGHEST, preferred_element_type=jnp.float32,
    )


def symmetric_inverse(a, b, c):
    scale = 1.0 / (a * c - b * b)
    return c * scale, -b * scale, a * scale


def pivot_inverse(e):
    a0, a1, a2 = symmetric_inverse(e[0][0], e[0][1], e[1][1])
    b00, b01, b10, b11 = e[0][2], e[0][3], e[1][2], e[1][3]
    f00, f01 = a0 * b00 + a1 * b10, a0 * b01 + a1 * b11
    f10, f11 = a1 * b00 + a2 * b10, a1 * b01 + a2 * b11
    s0, s1, s2 = symmetric_inverse(
        e[2][2] - (b00 * f00 + b10 * f10),
        e[2][3] - (b00 * f01 + b10 * f11),
        e[3][3] - (b01 * f01 + b11 * f11),
    )
    t00, t01 = f00 * s0 + f01 * s1, f00 * s1 + f01 * s2
    t10, t11 = f10 * s0 + f11 * s1, f10 * s1 + f11 * s2
    x01 = a1 + t00 * f10 + t01 * f11
    return [
        [a0 + t00 * f00 + t01 * f01, x01, -t00, -t01],
        [x01, a2 + t10 * f10 + t11 * f11, -t10, -t11],
        [-t00, -t10, s0, s1],
        [-t01, -t11, s1, s2],
    ]


def inverse(tiles):
    row = lax.broadcasted_iota(jnp.int32, (8, LANES), 0)
    lane = lane_index((8, LANES))
    size = 4

    def everywhere(block):
        return jnp.broadcast_to(block, (8, LANES))

    for k in range(0, ENSEMBLE, size):
        home, start = k // 8, k % 8
        columns = [[everywhere(tile[:, k + j : k + j + 1]) for tile in tiles] for j in range(size)]
        rows = [everywhere(tiles[home][start + i : start + i + 1]) for i in range(size)]
        pivots = pivot_inverse(
            [
                [everywhere(columns[j][home][start + i : start + i + 1]) for j in range(size)]
                for i in range(size)
            ]
        )
        scaled = []
        for i in range(size):
            value = (pivots[i][0] * rows[0] + pivots[i][1] * rows[1]) + (
                pivots[i][2] * rows[2] + pivots[i][3] * rows[3]
            )
            for j in range(size):
                value = jnp.where(lane == k + j, pivots[i][j], value)
            scaled.append(value)
        inside = (lane >= k) & (lane < k + size)
        rest = []
        for t, tile in enumerate(tiles):
            value = jnp.where(inside, 0.0, tile)
            for j in range(size):
                value = value - columns[j][t] * scaled[j]
            rest.append(value)
        for i in range(size):
            rest[home] = jnp.where(row == start + i, scaled[i], rest[home])
        tiles = rest
    return jnp.concatenate(tiles, 0)


def analyse(received, own, off_chip, on_chip, out):
    row = lax.broadcasted_iota(jnp.int32, (SYSTEM_ROWS, LANES), 0)
    diagonal = row == lane_index((SYSTEM_ROWS, LANES))
    identity = jnp.where(diagonal & (row < ENSEMBLE), 1.0, 0.0)
    system = identity + gram(received, (own, off_chip, on_chip))
    solved = inverse([system[8 * t : 8 * t + 8] for t in range(SYSTEM_ROWS // 8)])
    weights = 0.5 * (solved - identity)[:ENSEMBLE] - solved[ENSEMBLE : ENSEMBLE + 1]
    high, low = split(weights[:, :ENSEMBLE], 2)
    weights = jnp.concatenate([high, low, high], 1)
    for r in range(ROWS):
        members = jnp.concatenate(
            [
                received[:, first : first + MEMBERS, :].reshape(ENSEMBLE, LANES)
                for first in (r * MEMBERS, HALF_ROWS + r * MEMBERS)
            ],
            1,
        )
        mean = jnp.sum(members, 0, keepdims=True) / ENSEMBLE
        high, low = split(members - mean, 2)
        result = members + jnp.dot(
            weights, jnp.concatenate([high, high, low], 0), preferred_element_type=jnp.float32
        )
        for m in range(ENSEMBLE // MEMBERS):
            rows = result[m * MEMBERS : (m + 1) * MEMBERS]
            out[m, pl.ds(r, MEMBERS, stride=ROWS), :] = rows[:, :LANES]
            out[m, pl.ds(HALF_ROWS + r, MEMBERS, stride=ROWS), :] = rows[:, LANES:]


def unpack(planes, out, left):
    copies = []
    for q in range(PLANES):
        for half in range(2):
            copies.append(
                pltpu.make_async_copy(
                    planes.at[q, half],
                    out.at[:, q, :, half * LANES : (half + 1) * LANES],
                    left.at[q, half],
                )
            )
    for copy in copies:
        copy.start()
    for copy in copies:
        copy.wait()


def vmem():
    return pl.BlockSpec(memory_space=pltpu.VMEM)


def hbm():
    return pl.BlockSpec(memory_space=pltpu.HBM)


def kernel(
    body, operands, *shapes, scalars=(), fetched=(), scratch=(), out_spec=vmem, aliases={}
):
    fetched = [pltpu.with_memory_space_constraint(x, pltpu.HBM) for x in fetched]
    shapes = [s if hasattr(s, "dtype") else jax.ShapeDtypeStruct(s, jnp.float32) for s in shapes]
    return pl.pallas_call(
        body,
        out_shape=shapes,
        in_specs=[vmem()] * len(operands)
        + [pl.BlockSpec(memory_space=pltpu.SMEM)] * len(scalars)
        + [hbm()] * len(fetched),
        out_specs=[out_spec() for _ in shapes],
        scratch_shapes=scratch,
        input_output_aliases=aliases,
        compiler_params=PARAMS,
        name=body.__name__,
    )(*operands, *scalars, *fetched)


def swapped(value, start):
    count = lax.axis_size("tile")
    pairs = [((i + start) % count, (i + 1 + start) % count) for i in range(0, count, 2)]
    return lax.ppermute(value, "tile", pairs + [(b, a) for a, b in pairs])


def both_neighbours(off_chip, on_chip):
    far = swapped(off_chip, 1)
    return far, swapped(on_chip, 0)


def exchanged(value):
    return lax.all_to_all(value, "mem", split_axis=0, concat_axis=0, tiled=True)


def local(
    member_tracer_state, diffusivity, velocity, wet_mask, obs_cell, obs_count, obs_value, obs_error
):
    slot_rows = [x.reshape(1, SLOTS) for x in (obs_cell, obs_value, obs_error)]
    off_chip, on_chip, *blocks, cell, value, error = kernel(
        pack_edges,
        (),
        (ROWS, COLUMNS),
        (ROWS, COLUMNS),
        member_tracer_state.shape,
        (2 * LEVELS, ROWS, COLUMNS),
        jax.ShapeDtypeStruct((ROWS, COLUMNS), jnp.int32),
        jax.ShapeDtypeStruct((1, SLOTS), jnp.int32),
        (1, SLOTS),
        (1, SLOTS),
        fetched=(member_tracer_state, diffusivity, velocity, wet_mask, *slot_rows),
        scratch=[pltpu.SemaphoreType.DMA((PARTS + 6,))],
    )
    edges = (off_chip, on_chip, *both_neighbours(off_chip, on_chip))
    own, sides_of = kernel(
        observe,
        (*blocks, *edges, cell, value, error),
        (2 * MEMBERS, SLOTS),
        (2 * ROWS, LANES),
        scalars=(obs_count,),
    )
    near = (own, *both_neighbours(own, own))
    home = (*blocks, *edges, sides_of)
    (chunks,) = kernel(transport, home, (PLANES, CHUNK_ROWS, LANES))
    (chunks,) = kernel(attach, (chunks, *near, *home), chunks.shape, aliases={0: 0})
    received = exchanged(chunks)
    (updated,) = kernel(analyse, (received, *near), (PLANES, CELL_ROWS, LANES))
    back = exchanged(updated)
    (analysis,) = kernel(
        unpack,
        (back.reshape(PLANES, 2, MEMBERS, ROWS, LANES),),
        member_tracer_state.shape,
        scratch=[pltpu.SemaphoreType.DMA((PLANES, 2))],
        out_spec=hbm,
    )
    return analysis


def solution(mesh):
    in_specs = (
        P("mem", None, None, "tile"),
        P(None, None, "tile"),
        P(None, None, "tile"),
        P(None, "tile"),
        P("tile"),
        P("tile"),
        P("tile"),
        P("tile"),
    )
    out_specs = P("mem", None, None, "tile")
    return jax.shard_map(local, mesh=mesh, in_specs=in_specs, out_specs=out_specs, check_vma=False)
```

```python
import jax
import jax.numpy as jnp
from jax import lax
from jax.experimental import pallas as pl
from jax.experimental.pallas import tpu as pltpu
from jax.sharding import PartitionSpec as P

LEVELS = 4
PLANES = 8
MEMBERS = 8
PARTS = 4
ENSEMBLE = 64
ROWS = 16
COLUMNS = 256
SLOTS = 128
LANES = 128
HALF_ROWS = ROWS * MEMBERS
CELL_ROWS = 2 * HALF_ROWS
CHUNK_ROWS = CELL_ROWS + 3 * MEMBERS
SYSTEM_ROWS = ENSEMBLE + 8
TRACER_LANES, STATIC_LANES = slice(0, LANES), slice(LANES, 2 * LANES)
HIGHEST = lax.Precision.HIGHEST
PARAMS = pltpu.CompilerParams(vmem_limit_bytes=32 * 1024 * 1024)


def lane_index(shape):
    return lax.broadcasted_iota(jnp.int32, shape, 1)


def pack_edges(
    state, diffusivity, velocity, wet, cell, value, error, off_chip, on_chip, own_state, own_statics,
    own_wet, own_cell, own_value, own_error, arrived
):
    odd = lax.axis_index("tile") % 2 == 1

    def hand_out(lanes, first, last):
        on_chip[:, lanes] = jnp.where(odd, first, last)
        off_chip[:, lanes] = jnp.where(odd, last, first)

    copies = []
    for part in range(PARTS):
        rows = slice(part * MEMBERS // PARTS, (part + 1) * MEMBERS // PARTS)
        copies.append((state.at[rows], own_state.at[rows]))
    copies += [
        (diffusivity, own_statics.at[:LEVELS]),
        (velocity, own_statics.at[LEVELS:]),
        (wet, own_wet),
        (cell, own_cell),
        (value, own_value),
        (error, own_error),
    ]
    copies = [
        pltpu.make_async_copy(source, target, arrived.at[i])
        for i, (source, target) in enumerate(copies)
    ]
    for copy in copies:
        copy.start()
    pair = lane_index((ROWS, LANES)) >> 1

    def put(low, high, index, kept):
        first_kept, last_kept = kept
        first_kept = jnp.where(pair == index, pltpu.roll(low, 2 * index, 1), first_kept)
        last_kept = jnp.where(
            pair == index, pltpu.roll(high, (2 * index + 2) % LANES, 1), last_kept
        )
        return first_kept, last_kept

    def member(e, kept):
        for q in range(PLANES):
            low, high = own_state[e, q, :, :LANES], own_state[e, q, :, LANES:]
            kept = put(low, high, e * PLANES + q, kept)
        return kept

    zeros = jnp.zeros((ROWS, LANES), jnp.float32)
    kept = (zeros, zeros)
    for part in range(PARTS):
        copies[part].wait()
        rows = range(part * MEMBERS // PARTS, (part + 1) * MEMBERS // PARTS)
        for e in rows:
            kept = member(e, kept)
    hand_out(TRACER_LANES, *kept)
    for copy in copies[PARTS:]:
        copy.wait()
    kept = (zeros, zeros)
    for i in range(2 * LEVELS):
        kept = put(own_statics[i, :, :LANES], own_statics[i, :, LANES:], i, kept)
    flags = own_wet[...].astype(jnp.float32)
    kept = put(flags[:, :LANES], flags[:, LANES:], 2 * LEVELS, kept)
    hand_out(STATIC_LANES, *kept)


def sides(sent_off, sent_on, off_chip, on_chip, lanes):
    odd_block = lax.axis_index("tile") % 2 == 1
    off, on = off_chip[:, lanes], on_chip[:, lanes]
    west, east = jnp.where(odd_block, on, off), jnp.where(odd_block, off, on)
    off, on = sent_off[:, lanes], sent_on[:, lanes]
    own_first, own_last = jnp.where(odd_block, on, off), jnp.where(odd_block, off, on)
    odd = lane_index((ROWS, LANES)) % 2 == 1
    inner = jnp.where(odd, pltpu.roll(own_first, 1, 1), pltpu.roll(own_last, LANES - 1, 1))
    outer = jnp.where(odd, pltpu.roll(west, 1, 1), pltpu.roll(east, LANES - 1, 1))
    return inner, jnp.where(odd, west, east), outer


def repeated(block, start, width):
    lane = lane_index((ROWS, LANES))
    if start:
        block = pltpu.roll(block, LANES - start, 1)
    block = jnp.where(lane < width, block, 0.0)
    while width < LANES:
        block = block + pltpu.roll(block, width, 1)
        width *= 2
    return block


def face(wet, speed, diffuse):
    a = 0.5 * (speed[0] + speed[1])
    k = 0.5 * (diffuse[0] + diffuse[1])
    ocean = wet[0] * wet[1]
    return ocean * (jnp.maximum(a, 0.0) + k), ocean * (jnp.minimum(a, 0.0) - k)


def rows_between(wet, diffuse):
    row = lax.broadcasted_iota(jnp.int32, (ROWS, LANES), 0)
    both = wet * pltpu.roll(wet, ROWS - 1, 0)
    k = 0.5 * (diffuse + pltpu.roll(diffuse, ROWS - 1, 0))
    north = jnp.where(row < ROWS - 1, both * k, 0.0)
    return pltpu.roll(north, 1, 0), north


def five_point(weights, cell, west, east):
    centre, to_west, to_east, above, north = weights
    return (
        centre * cell
        + to_west * west
        + to_east * east
        + above * pltpu.roll(cell, 1, 0)
        + north * pltpu.roll(cell, ROWS - 1, 0)
    )


def border(edges):
    odd = lane_index((ROWS, LANES)) % 2 == 1
    inner, cell, outer = sides(*edges, TRACER_LANES)
    statics = sides(*edges, STATIC_LANES)
    diffuse = [repeated(x, 0, 2 * LEVELS) for x in statics]
    speed = [repeated(x, 2 * LEVELS, 2 * LEVELS) for x in statics]
    wet = [repeated(x, 4 * LEVELS, 2) for x in statics]
    in_west, in_east = face(wet[:2], speed[:2], diffuse[:2])
    out_west, out_east = face(wet[1:], speed[1:], diffuse[1:])
    above, north = rows_between(wet[1], diffuse[1])
    zonal = jnp.where(odd, out_east - in_west, in_east - out_west)
    centre = 1.0 + (zonal - above - north) * wet[1]
    to_inner = jnp.where(odd, -in_east, in_west)
    to_outer = jnp.where(odd, out_west, -out_east)
    stepped = five_point((centre, to_inner, to_outer, above, north), cell, inner, outer)
    return cell, stepped


def neighbours(tiles, halo):
    return bordered(
        [pltpu.roll(tile, 1, 1) for tile in tiles],
        [pltpu.roll(tile, LANES - 1, 1) for tile in tiles],
        halo,
    )


def bordered(west, east, halo):
    lane = lane_index((ROWS, LANES))
    first, last = lane == 0, lane == LANES - 1
    west = [jnp.where(first, halo, west[0]), jnp.where(first, west[0], west[1])]
    return west, [jnp.where(last, east[1], east[0]), jnp.where(last, halo, east[1])]


def turns():
    row = lax.broadcasted_iota(jnp.int32, (3 * LANES, 2 * LANES), 0)
    column = lax.broadcasted_iota(jnp.int32, (3 * LANES, 2 * LANES), 1)
    source = jnp.where(column < LANES, column + LANES - 1, column + 1) % LANES
    return (row % LANES == source).astype(jnp.bfloat16)


def split(block, count):
    parts = []
    for i in range(count):
        parts.append(block.astype(jnp.bfloat16))
        block = block - parts[-1].astype(jnp.float32)
    return parts


def aligned(block, index):
    return pltpu.roll(block, LANES - 1 - 2 * index, 1)


def halved(block):
    return [block[:, :LANES], block[:, LANES:]]


def stepper(level, statics, wet, edges):
    cells = sides(*edges, STATIC_LANES)[1]
    ocean = halved(wet[...].astype(jnp.float32))
    diffuse, speed = halved(statics[level]), halved(statics[LEVELS + level])
    (wet_west, wet_east), (diffuse_west, diffuse_east), (speed_west, speed_east) = (
        neighbours(tiles, aligned(cells, index))
        for tiles, index in ((ocean, 2 * LEVELS), (diffuse, level), (speed, LEVELS + level))
    )
    weights = []
    for i in range(2):
        west = face((wet_west[i], ocean[i]), (speed_west[i], speed[i]), (diffuse_west[i], diffuse[i]))
        east = face((ocean[i], wet_east[i]), (speed[i], speed_east[i]), (diffuse[i], diffuse_east[i]))
        above, north = rows_between(ocean[i], diffuse[i])
        centre = 1.0 + (west[1] - east[0] - above - north) * ocean[i]
        weights.append((centre, west[0], -east[1], above, north))

    return weights


def two_steps(weights, turn, planes, borders):
    count = len(planes) // 2
    for halos in borders:
        stacked = jnp.concatenate([tiles[half] for half in range(2) for tiles in planes[:count]], 0)
        moved = jnp.dot(
            jnp.concatenate(split(stacked, 3), 1), turn, preferred_element_type=jnp.float32
        )
        stepped = []
        for i, tiles in enumerate(planes):
            if i < count:
                turned = [
                    halved(moved[(half * count + i) * ROWS : (half * count + i + 1) * ROWS])
                    for half in range(2)
                ]
                west, east = bordered(*zip(*turned), halos[i])
            else:
                west, east = neighbours(tiles, halos[i])
            stepped.append([five_point(weights[h], tiles[h], west[h], east[h]) for h in range(2)])
        planes = stepped
    return planes


def forecast(state, statics, wet, sent_off, sent_on, off_chip, on_chip, sides_of, chunks):
    edges = (sent_off, sent_on, off_chip, on_chip)
    borders = (sides_of[:ROWS], sides_of[ROWS:])
    turn = turns()

    def level_step(level, carry):
        weights = stepper(level, statics, wet, edges)
        where = [(e, t * LEVELS + level) for e in range(MEMBERS) for t in range(2)]
        planes = [halved(state[e, q]) for e, q in where]
        halos = [[aligned(block, e * PLANES + q) for e, q in where] for block in borders]
        for (e, q), done in zip(where, two_steps(weights, turn, planes, halos)):
            for half in range(2):
                rows = pl.ds(half * HALF_ROWS + e, ROWS, stride=MEMBERS)
                chunks[q, rows, :] = done[half]
        return carry

    lax.fori_loop(0, LEVELS, level_step, 0)


def far():
    place = lax.axis_index("tile") % 4
    return (place == 0) | (place == 3)


def transport(*refs):
    @pl.when(jnp.logical_not(far()))
    def _():
        forecast(*refs)


def observe(
    state, statics, wet, sent_off, sent_on, off_chip, on_chip, cell, value, error, count, out, sides_of
):
    edges = (sent_off, sent_on, off_chip, on_chip)
    borders = border(edges)
    sides_of[:ROWS], sides_of[ROWS:] = borders
    weights = stepper(0, statics, wet, edges)
    planes = [halved(state[e, 0]) for e in range(MEMBERS)]
    halos = [[aligned(block, e * PLANES) for e in range(MEMBERS)] for block in borders]
    surface = [jnp.concatenate(x, 1) for x in two_steps(weights, turns(), planes, halos)]
    in_use = (lane_index((1, SLOTS)) < count[0]).astype(jnp.float32)
    scale = 1.0 / ((ENSEMBLE - 1) * error[...])
    unused = jnp.zeros((5, SLOTS), jnp.float32)
    out[MEMBERS:, :] = jnp.concatenate([in_use, value[...], scale, unused], 0)
    cell = cell[...]
    column = lax.broadcasted_iota(jnp.int32, (COLUMNS, SLOTS), 0)
    pick = (column == (cell & (COLUMNS - 1))).astype(jnp.float32)
    near = jnp.dot(
        jnp.concatenate(surface, 0), pick, precision=HIGHEST, preferred_element_type=jnp.float32
    )
    layer = lax.broadcasted_iota(jnp.int32, (ROWS, SLOTS), 0)
    chosen = layer == (cell >> 8)
    for e in range(MEMBERS):
        kept = jnp.where(chosen, near[e * ROWS : (e + 1) * ROWS], 0.0)
        out[e : e + 1, :] = jnp.sum(kept, 0, keepdims=True)


def attach(chunks, own, last_chip, off_chip, on_chip, *rest):
    out = rest[-1]

    @pl.when(far())
    def _():
        forecast(*rest)

    near = (own[:MEMBERS], off_chip[:MEMBERS], on_chip[:MEMBERS] + last_chip[:MEMBERS])
    for i, values in enumerate(near):
        for q in range(PLANES):
            out[q, pl.ds(CELL_ROWS + i * MEMBERS, MEMBERS), :] = values


def gram(received, blocks):
    first = lax.broadcasted_iota(jnp.int32, (8, SLOTS), 0) == 0
    unused = jnp.zeros((LANES - ENSEMBLE, SLOTS), jnp.float32)
    left, right = [], []
    for i, (block, locality) in enumerate(zip(blocks, (1.0, 0.5, 0.5))):
        rows = pl.ds(CELL_ROWS + i * MEMBERS, MEMBERS)
        members = received[:, rows, :].reshape(ENSEMBLE, SLOTS)
        in_use, value, scale = (block[MEMBERS + j : MEMBERS + j + 1] for j in range(3))
        mean = jnp.sum(members, 0, keepdims=True) / ENSEMBLE
        anomaly = (members - mean) * in_use
        innovation = (value - mean) * in_use
        left.append(jnp.concatenate([anomaly, jnp.where(first, innovation, 0.0)], 0))
        right.append(jnp.concatenate([anomaly * (scale * locality), unused], 0))
    return lax.dot_general(
        jnp.concatenate(left, 1), jnp.concatenate(right, 1), (((1,), (1,)), ((), ())),
        precision=HIGHEST, preferred_element_type=jnp.float32,
    )


def symmetric_inverse(a, b, c):
    scale = 1.0 / (a * c - b * b)
    return c * scale, -b * scale, a * scale


def pivot_inverse(e):
    a0, a1, a2 = symmetric_inverse(e[0][0], e[0][1], e[1][1])
    b00, b01, b10, b11 = e[0][2], e[0][3], e[1][2], e[1][3]
    f00, f01 = a0 * b00 + a1 * b10, a0 * b01 + a1 * b11
    f10, f11 = a1 * b00 + a2 * b10, a1 * b01 + a2 * b11
    s0, s1, s2 = symmetric_inverse(
        e[2][2] - (b00 * f00 + b10 * f10),
        e[2][3] - (b00 * f01 + b10 * f11),
        e[3][3] - (b01 * f01 + b11 * f11),
    )
    t00, t01 = f00 * s0 + f01 * s1, f00 * s1 + f01 * s2
    t10, t11 = f10 * s0 + f11 * s1, f10 * s1 + f11 * s2
    x01 = a1 + t00 * f10 + t01 * f11
    return [
        [a0 + t00 * f00 + t01 * f01, x01, -t00, -t01],
        [x01, a2 + t10 * f10 + t11 * f11, -t10, -t11],
        [-t00, -t10, s0, s1],
        [-t01, -t11, s1, s2],
    ]


def inverse(tiles):
    row = lax.broadcasted_iota(jnp.int32, (8, LANES), 0)
    lane = lane_index((8, LANES))
    size = 4

    def everywhere(block):
        return jnp.broadcast_to(block, (8, LANES))

    for k in range(0, ENSEMBLE, size):
        home, start = k // 8, k % 8
        columns = [[everywhere(tile[:, k + j : k + j + 1]) for tile in tiles] for j in range(size)]
        rows = [everywhere(tiles[home][start + i : start + i + 1]) for i in range(size)]
        pivots = pivot_inverse(
            [
                [everywhere(columns[j][home][start + i : start + i + 1]) for j in range(size)]
                for i in range(size)
            ]
        )
        scaled = []
        for i in range(size):
            value = (pivots[i][0] * rows[0] + pivots[i][1] * rows[1]) + (
                pivots[i][2] * rows[2] + pivots[i][3] * rows[3]
            )
            for j in range(size):
                value = jnp.where(lane == k + j, pivots[i][j], value)
            scaled.append(value)
        inside = (lane >= k) & (lane < k + size)
        rest = []
        for t, tile in enumerate(tiles):
            value = jnp.where(inside, 0.0, tile)
            for j in range(size):
                value = value - columns[j][t] * scaled[j]
            rest.append(value)
        for i in range(size):
            rest[home] = jnp.where(row == start + i, scaled[i], rest[home])
        tiles = rest
    return jnp.concatenate(tiles, 0)


def analyse(received, own, last_chip, off_chip, on_chip, out):
    row = lax.broadcasted_iota(jnp.int32, (SYSTEM_ROWS, LANES), 0)
    diagonal = row == lane_index((SYSTEM_ROWS, LANES))
    identity = jnp.where(diagonal & (row < ENSEMBLE), 1.0, 0.0)
    system = identity + gram(received, (own[...], off_chip[...], on_chip[...] + last_chip[...]))
    solved = inverse([system[8 * t : 8 * t + 8] for t in range(SYSTEM_ROWS // 8)])
    weights = 0.5 * (solved - identity)[:ENSEMBLE] - solved[ENSEMBLE : ENSEMBLE + 1]
    high, low = split(weights[:, :ENSEMBLE], 2)
    weights = jnp.concatenate([high, low, high], 1)
    for r in range(ROWS):
        members = jnp.concatenate(
            [
                received[:, first : first + MEMBERS, :].reshape(ENSEMBLE, LANES)
                for first in (r * MEMBERS, HALF_ROWS + r * MEMBERS)
            ],
            1,
        )
        mean = jnp.sum(members, 0, keepdims=True) / ENSEMBLE
        high, low = split(members - mean, 2)
        result = members + jnp.dot(
            weights, jnp.concatenate([high, high, low], 0), preferred_element_type=jnp.float32
        )
        for m in range(ENSEMBLE // MEMBERS):
            rows = result[m * MEMBERS : (m + 1) * MEMBERS]
            out[m, pl.ds(r, MEMBERS, stride=ROWS), :] = rows[:, :LANES]
            out[m, pl.ds(HALF_ROWS + r, MEMBERS, stride=ROWS), :] = rows[:, LANES:]


def unpack(planes, out, left):
    copies = []
    for q in range(PLANES):
        for half in range(2):
            copies.append(
                pltpu.make_async_copy(
                    planes.at[q, half],
                    out.at[:, q, :, half * LANES : (half + 1) * LANES],
                    left.at[q, half],
                )
            )
    for copy in copies:
        copy.start()
    for copy in copies:
        copy.wait()


def vmem():
    return pl.BlockSpec(memory_space=pltpu.VMEM)


def hbm():
    return pl.BlockSpec(memory_space=pltpu.HBM)


def kernel(
    body, operands, *shapes, scalars=(), fetched=(), scratch=(), out_spec=vmem, aliases={}
):
    fetched = [pltpu.with_memory_space_constraint(x, pltpu.HBM) for x in fetched]
    shapes = [s if hasattr(s, "dtype") else jax.ShapeDtypeStruct(s, jnp.float32) for s in shapes]
    return pl.pallas_call(
        body,
        out_shape=shapes,
        in_specs=[vmem()] * len(operands)
        + [pl.BlockSpec(memory_space=pltpu.SMEM)] * len(scalars)
        + [hbm()] * len(fetched),
        out_specs=[out_spec() for _ in shapes],
        scratch_shapes=scratch,
        input_output_aliases=aliases,
        compiler_params=PARAMS,
        name=body.__name__,
    )(*operands, *scalars, *fetched)


def swapped(value, start, stop):
    count = lax.axis_size("tile")
    pairs = [(i, (i + 1) % count) for i in range(start, stop, 2)]
    return lax.ppermute(value, "tile", pairs + [(b, a) for a, b in pairs])


def exchanged(value):
    return lax.all_to_all(value, "mem", split_axis=0, concat_axis=0, tiled=True)


def local(
    member_tracer_state, diffusivity, velocity, wet_mask, obs_cell, obs_count, obs_value, obs_error
):
    slot_rows = [x.reshape(1, SLOTS) for x in (obs_cell, obs_value, obs_error)]
    off_chip, on_chip, *blocks, cell, value, error = kernel(
        pack_edges,
        (),
        (ROWS, COLUMNS),
        (ROWS, COLUMNS),
        member_tracer_state.shape,
        (2 * LEVELS, ROWS, COLUMNS),
        jax.ShapeDtypeStruct((ROWS, COLUMNS), jnp.int32),
        jax.ShapeDtypeStruct((1, SLOTS), jnp.int32),
        (1, SLOTS),
        (1, SLOTS),
        fetched=(member_tracer_state, diffusivity, velocity, wet_mask, *slot_rows),
        scratch=[pltpu.SemaphoreType.DMA((PARTS + 6,))],
    )
    count = lax.axis_size("tile")
    edges = (off_chip, on_chip, swapped(off_chip, 1, count), swapped(on_chip, 0, count))
    own, sides_of = kernel(
        observe,
        (*blocks, *edges, cell, value, error),
        (2 * MEMBERS, SLOTS),
        (2 * ROWS, LANES),
        scalars=(obs_count,),
    )
    last_chip = swapped(own, count - 2, count)
    off_chip = swapped(own, 1, count)
    near = (own, last_chip, off_chip, swapped(own, 0, count - 2))
    home = (*blocks, *edges, sides_of)
    (chunks,) = kernel(transport, home, (PLANES, CHUNK_ROWS, LANES))
    (chunks,) = kernel(attach, (chunks, *near, *home), chunks.shape, aliases={0: 0})
    received = exchanged(chunks)
    (updated,) = kernel(analyse, (received, *near), (PLANES, CELL_ROWS, LANES))
    back = exchanged(updated)
    (analysis,) = kernel(
        unpack,
        (back.reshape(PLANES, 2, MEMBERS, ROWS, LANES),),
        member_tracer_state.shape,
        scratch=[pltpu.SemaphoreType.DMA((PLANES, 2))],
        out_spec=hbm,
    )
    return analysis


def solution(mesh):
    in_specs = (
        P("mem", None, None, "tile"),
        P(None, None, "tile"),
        P(None, None, "tile"),
        P(None, "tile"),
        P("tile"),
        P("tile"),
        P("tile"),
        P("tile"),
    )
    out_specs = P("mem", None, None, "tile")
    return jax.shard_map(local, mesh=mesh, in_specs=in_specs, out_specs=out_specs, check_vma=False)
```

```python
import jax
import jax.numpy as jnp
from jax import lax
from jax.experimental import pallas as pl
from jax.experimental.pallas import tpu as pltpu
from jax.sharding import PartitionSpec as P

LEVELS = 4
PLANES = 8
MEMBERS = 8
PARTS = 4
ENSEMBLE = 64
ROWS = 16
COLUMNS = 256
SLOTS = 128
LANES = 128
HALF_ROWS = ROWS * MEMBERS
CELL_ROWS = 2 * HALF_ROWS
CHUNK_ROWS = CELL_ROWS + 3 * MEMBERS
SYSTEM_ROWS = ENSEMBLE + 8
TRACER_LANES, STATIC_LANES = slice(0, LANES), slice(LANES, 2 * LANES)
HIGHEST = lax.Precision.HIGHEST
PARAMS = pltpu.CompilerParams(vmem_limit_bytes=32 * 1024 * 1024)


def lane_index(shape):
    return lax.broadcasted_iota(jnp.int32, shape, 1)


def pack_edges(
    state, diffusivity, velocity, wet, cell, value, error, off_chip, on_chip, own_state, own_statics,
    own_wet, own_cell, own_value, own_error, arrived
):
    odd = lax.axis_index("tile") % 2 == 1

    def hand_out(lanes, first, last):
        on_chip[:, lanes] = jnp.where(odd, first, last)
        off_chip[:, lanes] = jnp.where(odd, last, first)

    copies = []
    for part in range(PARTS):
        rows = slice(part * MEMBERS // PARTS, (part + 1) * MEMBERS // PARTS)
        copies.append((state.at[rows], own_state.at[rows]))
    copies += [
        (diffusivity, own_statics.at[:LEVELS]),
        (velocity, own_statics.at[LEVELS:]),
        (wet, own_wet),
        (cell, own_cell),
        (value, own_value),
        (error, own_error),
    ]
    copies = [
        pltpu.make_async_copy(source, target, arrived.at[i])
        for i, (source, target) in enumerate(copies)
    ]
    for copy in copies:
        copy.start()
    pair = lane_index((ROWS, LANES)) >> 1

    def put(low, high, index, kept):
        first_kept, last_kept = kept
        first_kept = jnp.where(pair == index, pltpu.roll(low, 2 * index, 1), first_kept)
        last_kept = jnp.where(
            pair == index, pltpu.roll(high, (2 * index + 2) % LANES, 1), last_kept
        )
        return first_kept, last_kept

    def member(e, kept):
        for q in range(PLANES):
            low, high = own_state[e, q, :, :LANES], own_state[e, q, :, LANES:]
            kept = put(low, high, e * PLANES + q, kept)
        return kept

    zeros = jnp.zeros((ROWS, LANES), jnp.float32)
    kept = (zeros, zeros)
    for part in range(PARTS):
        copies[part].wait()
        rows = range(part * MEMBERS // PARTS, (part + 1) * MEMBERS // PARTS)
        for e in rows:
            kept = member(e, kept)
    hand_out(TRACER_LANES, *kept)
    for copy in copies[PARTS:]:
        copy.wait()
    kept = (zeros, zeros)
    for i in range(2 * LEVELS):
        kept = put(own_statics[i, :, :LANES], own_statics[i, :, LANES:], i, kept)
    flags = own_wet[...].astype(jnp.float32)
    kept = put(flags[:, :LANES], flags[:, LANES:], 2 * LEVELS, kept)
    hand_out(STATIC_LANES, *kept)


def sides(sent_off, sent_on, off_chip, on_chip, lanes):
    odd_block = lax.axis_index("tile") % 2 == 1
    off, on = off_chip[:, lanes], on_chip[:, lanes]
    west, east = jnp.where(odd_block, on, off), jnp.where(odd_block, off, on)
    off, on = sent_off[:, lanes], sent_on[:, lanes]
    own_first, own_last = jnp.where(odd_block, on, off), jnp.where(odd_block, off, on)
    odd = lane_index((ROWS, LANES)) % 2 == 1
    inner = jnp.where(odd, pltpu.roll(own_first, 1, 1), pltpu.roll(own_last, LANES - 1, 1))
    outer = jnp.where(odd, pltpu.roll(west, 1, 1), pltpu.roll(east, LANES - 1, 1))
    return inner, jnp.where(odd, west, east), outer


def repeated(block, start, width):
    lane = lane_index((ROWS, LANES))
    if start:
        block = pltpu.roll(block, LANES - start, 1)
    block = jnp.where(lane < width, block, 0.0)
    while width < LANES:
        block = block + pltpu.roll(block, width, 1)
        width *= 2
    return block


def face(wet, speed, diffuse):
    a = 0.5 * (speed[0] + speed[1])
    k = 0.5 * (diffuse[0] + diffuse[1])
    ocean = wet[0] * wet[1]
    return ocean * (jnp.maximum(a, 0.0) + k), ocean * (jnp.minimum(a, 0.0) - k)


def rows_between(wet, diffuse):
    row = lax.broadcasted_iota(jnp.int32, (ROWS, LANES), 0)
    both = wet * pltpu.roll(wet, ROWS - 1, 0)
    k = 0.5 * (diffuse + pltpu.roll(diffuse, ROWS - 1, 0))
    north = jnp.where(row < ROWS - 1, both * k, 0.0)
    return pltpu.roll(north, 1, 0), north


def five_point(weights, cell, west, east):
    centre, to_west, to_east, above, north = weights
    return (
        centre * cell
        + to_west * west
        + to_east * east
        + above * pltpu.roll(cell, 1, 0)
        + north * pltpu.roll(cell, ROWS - 1, 0)
    )


def border(edges):
    odd = lane_index((ROWS, LANES)) % 2 == 1
    inner, cell, outer = sides(*edges, TRACER_LANES)
    statics = sides(*edges, STATIC_LANES)
    diffuse = [repeated(x, 0, 2 * LEVELS) for x in statics]
    speed = [repeated(x, 2 * LEVELS, 2 * LEVELS) for x in statics]
    wet = [repeated(x, 4 * LEVELS, 2) for x in statics]
    in_west, in_east = face(wet[:2], speed[:2], diffuse[:2])
    out_west, out_east = face(wet[1:], speed[1:], diffuse[1:])
    above, north = rows_between(wet[1], diffuse[1])
    zonal = jnp.where(odd, out_east - in_west, in_east - out_west)
    centre = 1.0 + (zonal - above - north) * wet[1]
    to_inner = jnp.where(odd, -in_east, in_west)
    to_outer = jnp.where(odd, out_west, -out_east)
    stepped = five_point((centre, to_inner, to_outer, above, north), cell, inner, outer)
    return cell, stepped


def neighbours(tiles, halo):
    return bordered(
        [pltpu.roll(tile, 1, 1) for tile in tiles],
        [pltpu.roll(tile, LANES - 1, 1) for tile in tiles],
        halo,
    )


def bordered(west, east, halo):
    lane = lane_index((ROWS, LANES))
    first, last = lane == 0, lane == LANES - 1
    west = [jnp.where(first, halo, west[0]), jnp.where(first, west[0], west[1])]
    return west, [jnp.where(last, east[1], east[0]), jnp.where(last, halo, east[1])]


def turns():
    row = lax.broadcasted_iota(jnp.int32, (3 * LANES, 2 * LANES), 0)
    column = lax.broadcasted_iota(jnp.int32, (3 * LANES, 2 * LANES), 1)
    source = jnp.where(column < LANES, column + LANES - 1, column + 1) % LANES
    return (row % LANES == source).astype(jnp.bfloat16)


def split(block, count):
    parts = []
    for i in range(count):
        parts.append(block.astype(jnp.bfloat16))
        block = block - parts[-1].astype(jnp.float32)
    return parts


def aligned(block, index):
    return pltpu.roll(block, LANES - 1 - 2 * index, 1)


def halved(block):
    return [block[:, :LANES], block[:, LANES:]]


def stepper(level, statics, wet, edges):
    cells = sides(*edges, STATIC_LANES)[1]
    ocean = halved(wet[...].astype(jnp.float32))
    diffuse, speed = halved(statics[level]), halved(statics[LEVELS + level])
    (wet_west, wet_east), (diffuse_west, diffuse_east), (speed_west, speed_east) = (
        neighbours(tiles, aligned(cells, index))
        for tiles, index in ((ocean, 2 * LEVELS), (diffuse, level), (speed, LEVELS + level))
    )
    weights = []
    for i in range(2):
        west = face((wet_west[i], ocean[i]), (speed_west[i], speed[i]), (diffuse_west[i], diffuse[i]))
        east = face((ocean[i], wet_east[i]), (speed[i], speed_east[i]), (diffuse[i], diffuse_east[i]))
        above, north = rows_between(ocean[i], diffuse[i])
        centre = 1.0 + (west[1] - east[0] - above - north) * ocean[i]
        weights.append((centre, west[0], -east[1], above, north))

    return weights


def two_steps(weights, turn, planes, borders):
    count = len(planes) // 2
    for halos in borders:
        stacked = jnp.concatenate([tiles[half] for half in range(2) for tiles in planes[:count]], 0)
        moved = jnp.dot(
            jnp.concatenate(split(stacked, 3), 1), turn, preferred_element_type=jnp.float32
        )
        stepped = []
        for i, tiles in enumerate(planes):
            if i < count:
                turned = [
                    halved(moved[(half * count + i) * ROWS : (half * count + i + 1) * ROWS])
                    for half in range(2)
                ]
                west, east = bordered(*zip(*turned), halos[i])
            else:
                west, east = neighbours(tiles, halos[i])
            stepped.append([five_point(weights[h], tiles[h], west[h], east[h]) for h in range(2)])
        planes = stepped
    return planes


def forecast(state, statics, wet, sent_off, sent_on, off_chip, on_chip, sides_of, chunks):
    edges = (sent_off, sent_on, off_chip, on_chip)
    borders = (sides_of[:ROWS], sides_of[ROWS:])
    turn = turns()

    def level_step(level, carry):
        weights = stepper(level, statics, wet, edges)
        where = [(e, t * LEVELS + level) for e in range(MEMBERS) for t in range(2)]
        planes = [halved(state[e, q]) for e, q in where]
        halos = [[aligned(block, e * PLANES + q) for e, q in where] for block in borders]
        for (e, q), done in zip(where, two_steps(weights, turn, planes, halos)):
            for half in range(2):
                rows = pl.ds(half * HALF_ROWS + e, ROWS, stride=MEMBERS)
                chunks[q, rows, :] = done[half]
        return carry

    lax.fori_loop(0, LEVELS, level_step, 0)


def far():
    place = lax.axis_index("tile") % 4
    return (place == 0) | (place == 3)


def transport(*refs):
    @pl.when(jnp.logical_not(far()))
    def _():
        forecast(*refs)


def observe(
    state, statics, wet, sent_off, sent_on, off_chip, on_chip, cell, value, error, count, out, sides_of
):
    edges = (sent_off, sent_on, off_chip, on_chip)
    borders = border(edges)
    sides_of[:ROWS], sides_of[ROWS:] = borders
    weights = stepper(0, statics, wet, edges)
    planes = [halved(state[e, 0]) for e in range(MEMBERS)]
    halos = [[aligned(block, e * PLANES) for e in range(MEMBERS)] for block in borders]
    surface = [jnp.concatenate(x, 1) for x in two_steps(weights, turns(), planes, halos)]
    in_use = (lane_index((1, SLOTS)) < count[0]).astype(jnp.float32)
    scale = 1.0 / ((ENSEMBLE - 1) * error[...])
    unused = jnp.zeros((5, SLOTS), jnp.float32)
    out[MEMBERS:, :] = jnp.concatenate([in_use, value[...], scale, unused], 0)
    cell = cell[...]
    column = lax.broadcasted_iota(jnp.int32, (COLUMNS, SLOTS), 0)
    pick = (column == (cell & (COLUMNS - 1))).astype(jnp.float32)
    near = jnp.dot(
        jnp.concatenate(surface, 0), pick, precision=HIGHEST, preferred_element_type=jnp.float32
    )
    layer = lax.broadcasted_iota(jnp.int32, (ROWS, SLOTS), 0)
    chosen = layer == (cell >> 8)
    for e in range(MEMBERS):
        kept = jnp.where(chosen, near[e * ROWS : (e + 1) * ROWS], 0.0)
        out[e : e + 1, :] = jnp.sum(kept, 0, keepdims=True)


def attach(chunks, own, last_chip, off_chip, on_chip, *rest):
    out = rest[-1]

    @pl.when(far())
    def _():
        forecast(*rest)

    near = (own[:MEMBERS], off_chip[:MEMBERS], on_chip[:MEMBERS] + last_chip[:MEMBERS])
    for i, values in enumerate(near):
        for q in range(PLANES):
            out[q, pl.ds(CELL_ROWS + i * MEMBERS, MEMBERS), :] = values


def gram(received, blocks):
    first = lax.broadcasted_iota(jnp.int32, (8, SLOTS), 0) == 0
    unused = jnp.zeros((LANES - ENSEMBLE, SLOTS), jnp.float32)
    left, right = [], []
    for i, (block, locality) in enumerate(zip(blocks, (1.0, 0.5, 0.5))):
        rows = pl.ds(CELL_ROWS + i * MEMBERS, MEMBERS)
        members = received[:, rows, :].reshape(ENSEMBLE, SLOTS)
        in_use, value, scale = (block[MEMBERS + j : MEMBERS + j + 1] for j in range(3))
        mean = jnp.sum(members, 0, keepdims=True) / ENSEMBLE
        anomaly = (members - mean) * in_use
        innovation = (value - mean) * in_use
        left.append(jnp.concatenate([anomaly, jnp.where(first, innovation, 0.0)], 0))
        right.append(jnp.concatenate([anomaly * (scale * locality), unused], 0))
    return lax.dot_general(
        jnp.concatenate(left, 1), jnp.concatenate(right, 1), (((1,), (1,)), ((), ())),
        precision=HIGHEST, preferred_element_type=jnp.float32,
    )


def symmetric_inverse(a, b, c):
    scale = 1.0 / (a * c - b * b)
    return c * scale, -b * scale, a * scale


def pivot_inverse(e):
    a0, a1, a2 = symmetric_inverse(e[0][0], e[0][1], e[1][1])
    b00, b01, b10, b11 = e[0][2], e[0][3], e[1][2], e[1][3]
    f00, f01 = a0 * b00 + a1 * b10, a0 * b01 + a1 * b11
    f10, f11 = a1 * b00 + a2 * b10, a1 * b01 + a2 * b11
    s0, s1, s2 = symmetric_inverse(
        e[2][2] - (b00 * f00 + b10 * f10),
        e[2][3] - (b00 * f01 + b10 * f11),
        e[3][3] - (b01 * f01 + b11 * f11),
    )
    t00, t01 = f00 * s0 + f01 * s1, f00 * s1 + f01 * s2
    t10, t11 = f10 * s0 + f11 * s1, f10 * s1 + f11 * s2
    x01 = a1 + t00 * f10 + t01 * f11
    return [
        [a0 + t00 * f00 + t01 * f01, x01, -t00, -t01],
        [x01, a2 + t10 * f10 + t11 * f11, -t10, -t11],
        [-t00, -t10, s0, s1],
        [-t01, -t11, s1, s2],
    ]


def inverse(tiles, beside):
    row = lax.broadcasted_iota(jnp.int32, (8, LANES), 0)
    lane = lane_index((8, LANES))
    size = 4

    def everywhere(block):
        return jnp.broadcast_to(block, (8, LANES))

    for k in range(0, ENSEMBLE, size):
        home, start = k // 8, k % 8
        beside(k // size)
        columns = [[everywhere(tile[:, k + j : k + j + 1]) for tile in tiles] for j in range(size)]
        rows = [everywhere(tiles[home][start + i : start + i + 1]) for i in range(size)]
        pivots = pivot_inverse(
            [
                [everywhere(columns[j][home][start + i : start + i + 1]) for j in range(size)]
                for i in range(size)
            ]
        )
        scaled = []
        for i in range(size):
            value = (pivots[i][0] * rows[0] + pivots[i][1] * rows[1]) + (
                pivots[i][2] * rows[2] + pivots[i][3] * rows[3]
            )
            for j in range(size):
                value = jnp.where(lane == k + j, pivots[i][j], value)
            scaled.append(value)
        inside = (lane >= k) & (lane < k + size)
        rest = []
        for t, tile in enumerate(tiles):
            value = jnp.where(inside, 0.0, tile)
            for j in range(size):
                value = value - columns[j][t] * scaled[j]
            rest.append(value)
        for i in range(size):
            rest[home] = jnp.where(row == start + i, scaled[i], rest[home])
        tiles = rest
    return jnp.concatenate(tiles, 0)


def analyse(received, own, last_chip, off_chip, on_chip, out, parts):
    row = lax.broadcasted_iota(jnp.int32, (SYSTEM_ROWS, LANES), 0)
    diagonal = row == lane_index((SYSTEM_ROWS, LANES))
    identity = jnp.where(diagonal & (row < ENSEMBLE), 1.0, 0.0)
    system = identity + gram(received, (own[...], off_chip[...], on_chip[...] + last_chip[...]))

    def members_of(r):
        halves = [
            received[:, first : first + MEMBERS, :].reshape(ENSEMBLE, LANES)
            for first in (r * MEMBERS, HALF_ROWS + r * MEMBERS)
        ]
        return jnp.concatenate(halves, 1)

    def prepare(r):
        members = members_of(r)
        mean = jnp.sum(members, 0, keepdims=True) / ENSEMBLE
        high, low = split(members - mean, 2)
        parts[r] = jnp.concatenate([high, high, low], 0)

    solved = inverse([system[8 * t : 8 * t + 8] for t in range(SYSTEM_ROWS // 8)], prepare)
    weights = 0.5 * (solved - identity)[:ENSEMBLE] - solved[ENSEMBLE : ENSEMBLE + 1]
    high, low = split(weights[:, :ENSEMBLE], 2)
    weights = jnp.concatenate([high, low, high], 1)
    for r in range(ROWS):
        result = members_of(r) + jnp.dot(
            weights, parts[r], preferred_element_type=jnp.float32
        )
        for m in range(ENSEMBLE // MEMBERS):
            rows = result[m * MEMBERS : (m + 1) * MEMBERS]
            out[m, pl.ds(r, MEMBERS, stride=ROWS), :] = rows[:, :LANES]
            out[m, pl.ds(HALF_ROWS + r, MEMBERS, stride=ROWS), :] = rows[:, LANES:]


def unpack(planes, out, left):
    copies = []
    for q in range(PLANES):
        for half in range(2):
            copies.append(
                pltpu.make_async_copy(
                    planes.at[q, half],
                    out.at[:, q, :, half * LANES : (half + 1) * LANES],
                    left.at[q, half],
                )
            )
    for copy in copies:
        copy.start()
    for copy in copies:
        copy.wait()


def vmem():
    return pl.BlockSpec(memory_space=pltpu.VMEM)


def hbm():
    return pl.BlockSpec(memory_space=pltpu.HBM)


def kernel(
    body, operands, *shapes, scalars=(), fetched=(), scratch=(), out_spec=vmem, aliases={}
):
    fetched = [pltpu.with_memory_space_constraint(x, pltpu.HBM) for x in fetched]
    shapes = [s if hasattr(s, "dtype") else jax.ShapeDtypeStruct(s, jnp.float32) for s in shapes]
    return pl.pallas_call(
        body,
        out_shape=shapes,
        in_specs=[vmem()] * len(operands)
        + [pl.BlockSpec(memory_space=pltpu.SMEM)] * len(scalars)
        + [hbm()] * len(fetched),
        out_specs=[out_spec() for _ in shapes],
        scratch_shapes=scratch,
        input_output_aliases=aliases,
        compiler_params=PARAMS,
        name=body.__name__,
    )(*operands, *scalars, *fetched)


def swapped(value, start, stop):
    count = lax.axis_size("tile")
    pairs = [(i, (i + 1) % count) for i in range(start, stop, 2)]
    return lax.ppermute(value, "tile", pairs + [(b, a) for a, b in pairs])


def exchanged(value):
    return lax.all_to_all(value, "mem", split_axis=0, concat_axis=0, tiled=True)


def local(
    member_tracer_state, diffusivity, velocity, wet_mask, obs_cell, obs_count, obs_value, obs_error
):
    slot_rows = [x.reshape(1, SLOTS) for x in (obs_cell, obs_value, obs_error)]
    off_chip, on_chip, *blocks, cell, value, error = kernel(
        pack_edges,
        (),
        (ROWS, COLUMNS),
        (ROWS, COLUMNS),
        member_tracer_state.shape,
        (2 * LEVELS, ROWS, COLUMNS),
        jax.ShapeDtypeStruct((ROWS, COLUMNS), jnp.int32),
        jax.ShapeDtypeStruct((1, SLOTS), jnp.int32),
        (1, SLOTS),
        (1, SLOTS),
        fetched=(member_tracer_state, diffusivity, velocity, wet_mask, *slot_rows),
        scratch=[pltpu.SemaphoreType.DMA((PARTS + 6,))],
    )
    count = lax.axis_size("tile")
    edges = (off_chip, on_chip, swapped(off_chip, 1, count), swapped(on_chip, 0, count))
    own, sides_of = kernel(
        observe,
        (*blocks, *edges, cell, value, error),
        (2 * MEMBERS, SLOTS),
        (2 * ROWS, LANES),
        scalars=(obs_count,),
    )
    last_chip = swapped(own, count - 2, count)
    off_chip = swapped(own, 1, count)
    near = (own, last_chip, off_chip, swapped(own, 0, count - 2))
    home = (*blocks, *edges, sides_of)
    (chunks,) = kernel(transport, home, (PLANES, CHUNK_ROWS, LANES))
    (chunks,) = kernel(attach, (chunks, *near, *home), chunks.shape, aliases={0: 0})
    received = exchanged(chunks)
    (updated,) = kernel(
        analyse,
        (received, *near),
        (PLANES, CELL_ROWS, LANES),
        scratch=[pltpu.VMEM((ROWS, 3 * ENSEMBLE, COLUMNS), jnp.bfloat16)],
    )
    back = exchanged(updated)
    (analysis,) = kernel(
        unpack,
        (back.reshape(PLANES, 2, MEMBERS, ROWS, LANES),),
        member_tracer_state.shape,
        scratch=[pltpu.SemaphoreType.DMA((PLANES, 2))],
        out_spec=hbm,
    )
    return analysis


def solution(mesh):
    in_specs = (
        P("mem", None, None, "tile"),
        P(None, None, "tile"),
        P(None, None, "tile"),
        P(None, "tile"),
        P("tile"),
        P("tile"),
        P("tile"),
        P("tile"),
    )
    out_specs = P("mem", None, None, "tile")
    return jax.shard_map(local, mesh=mesh, in_specs=in_specs, out_specs=out_specs, check_vma=False)
```
